256 devices in a mesh: animal: 32 (over z, y), snp: 8 (over x, core).
Axes of the slice: x: 4, y: 4, z: 8, core: 2. Of those that a mesh axis runs over, the one named last changes fastest.
Arguments:
- genotype: bfloat16 [32768, 32768], P('animal', 'snp')
- allele_freq: float32 [32768], P('snp')
- right_side: float32 [32768, 128], P('animal'), may hold values from -6 to 6
- diagonal: float32 [32768, 128], P('animal'), may hold values from 0.5 to 2
- mendelian: float32 [32768], P('animal'), may hold values from 2 to 4
- genomic_weight: float32 [128], replicated, may hold values from 1 to 8
- send_rows: int32 [32, 32, 64], P('animal'), may hold values from 0 to 1023, as said below
- sire_slot: int32 [32768], P('animal'), may hold values from 0 to 1999, as said below
- dam_slot: int32 [32768], P('animal'), may hold values from 16 to 2047, as said below
Outputs:
- solution: float32 [32768, 128], P('animal')
- residual: float32 [32768, 128], P('animal')
The draws below stay inside these ranges and needn't reach their ends.
Inputs may be any that keep to these rules, and one draw needn't show every extreme that they name: send_rows[o, d, :] lists 64 distinct local rows of owner o's 1024 animals, those sent to device d. sire_slot[i] = o * 64 + k with k < 16. dam_slot[i] = o * 64 + k with k >= 16.
All inputs are finite; a program needn't handle non-finite values.
Results may differ from the reference program's by a relative error of at most 0.0067.
Values may be sent and summed in bfloat16 or wider, within the bound.
A program may use at most 64 MiB of HBM per device.

```python
import math
import jax
import jax.numpy as jnp
from jax import lax

ROWS_DEV = 1024
SNPS = 32768
SLOTS = 64
ITERS = 2
COLS = 128
OWNERS = 32
ANIMALS = 32768


def column_percent(key):
    return jax.random.randint(jax.random.fold_in(key, 11), (SNPS,), 5, 51)


def draw_allele_freq(key, part):
    return column_percent(key).astype(jnp.float32) / 100.0


def draw_genotype(key, part):
    percent = column_percent(key)
    joined = jax.random.randint(jax.random.fold_in(key, 12), (ANIMALS, SNPS), 0, 10000)
    first = joined % 100 < percent[None, :]
    second = joined // 100 < percent[None, :]
    codes = first.astype(jnp.int32) + second.astype(jnp.int32)
    return codes.astype(jnp.float32).astype(jnp.bfloat16)


def pedigree_plan(key):
    base = jax.random.fold_in(key, 21)
    scores = jax.random.randint(jax.random.fold_in(base, 1), (OWNERS, OWNERS, ROWS_DEV), 0, 65536)
    scores = scores * ROWS_DEV + jnp.arange(ROWS_DEV, dtype=jnp.int32)[None, None, :]
    order = jnp.argsort(scores, axis=-1)
    send = order[:, :, :SLOTS].astype(jnp.int32)
    first_src = jax.random.randint(jax.random.fold_in(base, 2), (ANIMALS,), 0, OWNERS)
    second_src = jax.random.randint(jax.random.fold_in(base, 3), (ANIMALS,), 0, OWNERS)
    sire_src = jnp.minimum(first_src, second_src)
    sire_within = jax.random.randint(jax.random.fold_in(base, 4), (ANIMALS,), 0, SLOTS // 4)
    dam_src = jax.random.randint(jax.random.fold_in(base, 5), (ANIMALS,), 0, OWNERS)
    dam_within = jax.random.randint(jax.random.fold_in(base, 6), (ANIMALS,), SLOTS // 4, SLOTS)
    sire = (sire_src * SLOTS + sire_within).astype(jnp.int32)
    dam = (dam_src * SLOTS + dam_within).astype(jnp.int32)
    return (send, sire, dam)


def draw_send_rows(key, part):
    return pedigree_plan(key)[0]


def draw_sire_slot(key, part):
    return pedigree_plan(key)[1]


def draw_dam_slot(key, part):
    return pedigree_plan(key)[2]


def block_scale(stream_key, dims, split, low, top_value):
    gain, own = 1.0, jax.random.fold_in(stream_key, 6)
    for position, blocks in split:
        heights = jnp.exp(jax.random.uniform(jax.random.fold_in(own, position), (blocks,), jnp.float32, low / len(split), top_value / len(split)))
        gain = gain * jnp.repeat(heights, dims[position] // blocks).reshape([-1 if axis == position else 1 for axis in range(len(dims))])
    return gain


def bell_draw(rng, extent, spread, bound, shards=(), kind=jnp.bfloat16):
    loudness = block_scale(rng, extent, shards, -0.22, 0.18) if shards else 1.0
    result = jax.random.normal(rng, extent, jnp.float32) * spread * loudness
    return jnp.minimum(jnp.maximum(result, -bound), bound).astype(kind)


def setup_inputs(seed: int = 0) -> dict:
    keys = jax.random.split(jax.random.key(seed), 10)
    genotype = draw_genotype(jax.random.fold_in(keys[9], 71), 0)
    allele_freq = draw_allele_freq(jax.random.fold_in(keys[9], 71), 0)
    right_side = bell_draw(keys[2], (ANIMALS, COLS), 1.0, 6.0, ((0, 32),), jnp.float32)
    diagonal = jnp.clip(jnp.exp(math.log(2.0) - 1.3862944 * jax.random.uniform(keys[3], (ANIMALS, COLS), jnp.float32) ** block_scale(keys[3], (ANIMALS, COLS), ((0, 32),), -0.2, 0.2)), 0.5, 2.0)
    mendelian = jnp.clip(2.0 + 2.0 * jax.random.uniform(keys[4], (ANIMALS,), jnp.float32) ** block_scale(keys[4], (ANIMALS,), ((0, 32),), -0.2, 0.2), 2.0, 4.0)
    genomic_weight = jnp.clip(jnp.exp(jax.random.uniform(keys[5], (COLS,), jnp.float32, math.log(1.0), math.log(8.0))), 1.0, 8.0)
    send_rows = draw_send_rows(jax.random.fold_in(keys[9], 71), 0)
    sire_slot = draw_sire_slot(jax.random.fold_in(keys[9], 71), 0)
    dam_slot = draw_dam_slot(jax.random.fold_in(keys[9], 71), 0)
    return dict(genotype=genotype, allele_freq=allele_freq, right_side=right_side, diagonal=diagonal, mendelian=mendelian, genomic_weight=genomic_weight, send_rows=send_rows, sire_slot=sire_slot, dam_slot=dam_slot)


def reference(genotype, allele_freq, right_side, diagonal, mendelian, genomic_weight, send_rows, sire_slot, dam_slot):
    centered = (genotype.astype(jnp.float32) - 2.0 * allele_freq[None, :]).astype(jnp.bfloat16)
    owner = (jnp.arange(ANIMALS) // ROWS_DEV).astype(jnp.int32)

    def parent(slot):
        source = slot // SLOTS
        within = slot % SLOTS
        return (source * ROWS_DEV + send_rows[source, owner, within]).astype(jnp.int32)

    sire = parent(sire_slot)
    dam = parent(dam_slot)
    scale = genomic_weight[None, :] / SNPS

    def operate(field):
        field_b = field.astype(jnp.bfloat16)
        effects = lax.dot_general(centered, field_b, (((0,), (0,)), ((), ())), preferred_element_type=jnp.float32)
        effects = effects.astype(jnp.bfloat16)
        genomic = jnp.dot(centered, effects, preferred_element_type=jnp.float32)
        mendel_term = mendelian[:, None] * (field - 0.5 * (field[sire] + field[dam]))
        pedigree = mendel_term + jnp.zeros_like(field).at[sire].add(-0.5 * mendel_term).at[dam].add(-0.5 * mendel_term)
        return diagonal * field + pedigree + scale * genomic

    solution = jnp.zeros_like(right_side)
    residual = right_side
    w_field = operate(residual)
    z_field = jnp.zeros_like(right_side)
    s_field = jnp.zeros_like(right_side)
    p_field = jnp.zeros_like(right_side)
    gamma_prev = None
    alpha_prev = None
    for step in range(ITERS):
        gamma = jnp.sum(residual * residual, axis=0)
        delta = jnp.sum(w_field * residual, axis=0)
        q_field = operate(w_field)
        if step == 0:
            beta = jnp.zeros_like(gamma)
            alpha = gamma / delta
        else:
            beta = gamma / gamma_prev
            alpha = gamma / (delta - beta * gamma / alpha_prev)
        z_field = q_field + beta * z_field
        s_field = w_field + beta * s_field
        p_field = residual + beta * p_field
        solution = solution + alpha * p_field
        residual = residual - alpha * s_field
        w_field = w_field - alpha * z_field
        gamma_prev = gamma
        alpha_prev = alpha
    return solution, residual
```

```python
import functools

import jax
import jax.numpy as jnp
from jax import lax
from jax.experimental import pallas as pl
from jax.experimental.pallas import tpu as pltpu
from jax.sharding import PartitionSpec as P

MESH = pl.DeviceIdType.MESH
SNPS = 32768
Z, Y, S = 8, 4, 8
OWN = Z * Y
COLS, ROWS, LOCAL = 128, 1024, 4096
SHARE = COLS // S
ZSHARE = COLS // Z
YCH = LOCAL // Y
SUBS = 2
SUB = YCH // SUBS
SLOTS = 64
NT = (((1,), (1,)), ((), ()))
F32, BF16 = jnp.float32, jnp.bfloat16


def dot(a, b):
    return jnp.dot(a, b, preferred_element_type=F32)


def dot_nt(a, b):
    return lax.dot_general(a, b, NT, preferred_element_type=F32)


def halves(value):
    high = value.astype(BF16)
    low = (value - high.astype(F32)).astype(BF16)
    return jnp.concatenate([high, low], axis=0)


def swap(value):
    return pltpu.roll(value, SLOTS, 1)


def kernel(
    geno, freq, rhs, diag, mend, weight, rows, sire, dam,
    x_out, r_out,
    block, send_hot, parent_hot, field, field_t, diag_t,
    y_own, y_send, y_recv, z_own, z_send, z_recv, effects,
    g_own, g_send, g_recv, p_send, p_recv, p_mat, dot_send, dot_recv, final,
    load_sem, y_s, y_r, z_s, z_r, zg_s, zg_r, yg_s, yg_r, g_s, g_r, x_s, x_r,
    p_s, p_r, d_s, d_r, f_s, f_r,
):
    a, s = lax.axis_index("animal"), lax.axis_index("snp")
    z, y = a // Y, a % Y

    def at_y(k):
        return (z * Y + (y + k) % Y, s)

    def at_z(k):
        return (((z + k) % Z) * Y + y, s)

    def at_s(k):
        return (a, (s + k) % S)

    def at_a(k):
        return ((a + k) % OWN, s)

    def remote(src, dst, send_sem, recv_sem, peer):
        return pltpu.make_async_remote_copy(
            src_ref=src, dst_ref=dst, send_sem=send_sem, recv_sem=recv_sem,
            device_id=peer, device_id_type=MESH,
        )

    def settle(ref, send_sem, recv_sem, peer):
        return remote(ref, ref, send_sem, recv_sem, peer)

    def y_lanes(which, sub):
        return pl.ds(pl.multiple_of(which * YCH + sub * SUB, SUB), SUB)

    def loads(which):
        lanes = pl.ds(pl.multiple_of(which * YCH, YCH), YCH)
        return pltpu.make_async_copy(geno.at[:, lanes], block.at[:, lanes], load_sem.at[which])

    for k in range(1, Y + 1):
        loads((y + k) % Y).start()

    barrier = pltpu.get_barrier_semaphore()

    def greet_a(k, carry):
        pl.semaphore_signal(barrier, inc=1, device_id=at_a(k), device_id_type=MESH)
        return carry

    def greet_s(k, carry):
        pl.semaphore_signal(barrier, inc=1, device_id=at_s(k), device_id_type=MESH)
        return carry

    lax.fori_loop(1, OWN, greet_a, 0)
    lax.fori_loop(1, S, greet_s, 0)

    field_t[...] = rhs[...].T
    diag_t[...] = diag[...].T
    field[0] = field_t[...].astype(BF16)
    mine = pl.ds(pl.multiple_of(s * SHARE, SHARE), SHARE)
    z_mine = pl.ds(pl.multiple_of(z * ZSHARE, ZSHARE), ZSHARE)
    b_share = field_t[mine, :]
    d_share = diag_t[mine, :]
    scale = weight[mine, :] * (1.0 / SNPS)
    lane = lax.broadcasted_iota(jnp.int32, (SHARE, 2 * SLOTS), 1)
    first = lane < SLOTS

    pl.semaphore_wait(barrier, OWN - 1 + S - 1)

    def centre(which):
        loads(which).wait()

        def rows_of(i, carry):
            at = pl.ds(pl.multiple_of(i * 64, 64), 64)
            lanes = pl.ds(pl.multiple_of(which * YCH, YCH), YCH)
            block[at, lanes] = (block[at, lanes].astype(F32) - 2.0 * freq[:, lanes]).astype(BF16)
            return carry

        lax.fori_loop(0, ROWS // 64, rows_of, 0)

    def effects_out(op):
        def one(k, carry):
            which = (y + k) % Y
            if op == 0:
                centre(which)

            def part(sub, inner):
                here = pl.ds(pl.multiple_of(sub * SUB, SUB), SUB)
                value = dot(field[op], block[:, y_lanes(which, sub)])
                y_send[op, which, :, here] = value.astype(BF16)
                remote(
                    y_send.at[op, which, :, here], y_recv.at[op, y, :, here],
                    y_s.at[op, k - 1, sub], y_r.at[op, y, sub], at_y(k),
                ).start()
                return inner

            lax.fori_loop(0, SUBS, part, 0)
            return carry

        lax.fori_loop(1, Y, one, 0)
        if op == 0:
            centre(y)
        for sub in range(SUBS):
            y_own[:, sub * SUB : (sub + 1) * SUB] = dot(field[op], block[:, y_lanes(y, sub)])

    def effects_mid(op):
        for sub in range(SUBS):
            here = slice(sub * SUB, (sub + 1) * SUB)
            total = y_own[:, here]
            for k in range(1, Y):
                which = (y + k) % Y
                piece = y_recv.at[op, which, :, here]
                settle(piece, y_s.at[op, k - 1, sub], y_r.at[op, which, sub], at_y(k)).wait_recv()
                total = total + piece[...].astype(F32)
            z_own[:, here] = total
            z_send[op, :, here] = total.astype(BF16)

            def give(k, carry):
                peer_rows = pl.ds(pl.multiple_of(((z + k) % Z) * ZSHARE, ZSHARE), ZSHARE)
                remote(
                    z_send.at[op, peer_rows, here], z_recv.at[op, z, :, here],
                    z_s.at[op, sub], z_r.at[op, sub], at_z(k),
                ).start()
                return carry

            lax.fori_loop(1, Z, give, 0)

    def effects_sum(op):
        for sub in range(SUBS):
            here = slice(sub * SUB, (sub + 1) * SUB)
            settle(
                z_recv.at[op, 0 : Z - 1, :, here], z_s.at[op, sub], z_r.at[op, sub], at_z(1)
            ).wait_recv()
            total = z_own[z_mine, here]
            for k in range(1, Z):
                total = total + z_recv[op, (z + k) % Z, :, here].astype(F32)
            effects[op, z_mine, y_lanes(y, sub)] = total.astype(BF16)

            def give(k, carry):
                piece = effects.at[op, z_mine, y_lanes(y, sub)]
                remote(piece, piece, zg_s.at[op, sub], zg_r.at[op, sub], at_z(k)).start()
                return carry

            lax.fori_loop(1, Z, give, 0)

    def effects_spread(op):
        for sub in range(SUBS):
            settle(
                effects.at[op, 0 : COLS - ZSHARE, y_lanes(y, sub)],
                zg_s.at[op, sub], zg_r.at[op, sub], at_z(1),
            ).wait_recv()
            for k in range(1, Y):
                piece = effects.at[op, :, y_lanes(y, sub)]
                remote(
                    piece, piece, yg_s.at[op, k - 1, sub], yg_r.at[op, y, sub], at_y(k)
                ).start()

    def genomic_own(op):
        lanes = pl.ds(pl.multiple_of(y * YCH, YCH), YCH)
        g_own[...] = dot_nt(effects[op, :, lanes], block[:, lanes])

    def genomic(op):
        for sub in range(SUBS):
            for k in range(1, Y):
                which = (y + k) % Y
                lanes = y_lanes(which, sub)
                piece = effects.at[op, :, lanes]
                settle(piece, yg_s.at[op, k - 1, sub], yg_r.at[op, which, sub], at_y(k)).wait_recv()
                g_own[...] += dot_nt(piece[...], block[:, lanes])
        g_send[op] = g_own[...].astype(BF16)

        def give(k, carry):
            peer_rows = pl.ds(pl.multiple_of(((s + k) % S) * SHARE, SHARE), SHARE)
            remote(
                g_send.at[op, peer_rows, :], g_recv.at[op, s], g_s.at[op], g_r.at[op], at_s(k)
            ).start()
            return carry

        lax.fori_loop(1, S, give, 0)
        settle(g_recv.at[op, 0 : S - 1], g_s.at[op], g_r.at[op], at_s(1)).wait_recv()
        total = g_own[mine, :]
        for k in range(1, S):
            total = total + g_recv[op, (s + k) % S].astype(F32)
        return total

    def relay_out(leg, op, value):
        both = value
        for pair in range(OWN // 2):
            lanes = slice(pair * 2 * SLOTS, (pair + 1) * 2 * SLOTS)
            high, low = both[:SHARE, lanes], both[SHARE:, lanes]
            p_send[op, leg, 2 * pair] = jnp.where(first, high, swap(low)).astype(BF16)
            p_send[op, leg, 2 * pair + 1] = jnp.where(first, swap(high), low).astype(BF16)

        def give(k, carry):
            peer = (a + k) % OWN
            remote(
                p_send.at[op, leg, peer], p_recv.at[op, leg, a],
                p_s.at[op, leg], p_r.at[op, leg], at_a(k),
            ).start()
            return carry

        lax.fori_loop(1, OWN, give, 0)

    def relay_in(leg, op):
        settle(
            p_recv.at[op, leg, 0 : OWN - 1], p_s.at[op, leg], p_r.at[op, leg], at_a(1)
        ).wait_recv()
        p_recv[op, leg, a] = p_send[op, leg, a]
        for pair in range(OWN // 2):
            lanes = slice(pair * 2 * SLOTS, (pair + 1) * 2 * SLOTS)
            one = p_recv[op, leg, 2 * pair].astype(F32)
            two = p_recv[op, leg, 2 * pair + 1].astype(F32)
            p_mat[:SHARE, lanes] = jnp.where(first, one, swap(two)).astype(BF16)
            p_mat[SHARE:, lanes] = jnp.where(first, swap(one), two).astype(BF16)
        return p_mat[...]

    def fold(both):
        return both[:SHARE] + both[SHARE:]

    def make_send_hot():
        even = rows[pl.ds(0, OWN // 2, stride=2), :]
        odd = rows[pl.ds(1, OWN // 2, stride=2), :]
        pairs = jnp.concatenate([even, odd], axis=1)
        at = lax.broadcasted_iota(jnp.int32, (ROWS, 2 * SLOTS), 0)
        for pair in range(OWN // 2):
            lanes = slice(pair * 2 * SLOTS, (pair + 1) * 2 * SLOTS)
            send_hot[:, lanes] = (at == pairs[pair : pair + 1, :]).astype(F32).astype(BF16)

    def make_parent_hot():
        def some(i, carry):
            at = lax.broadcasted_iota(jnp.int32, (128, ROWS), 0) + i * 128
            here = (at == sire[...]) | (at == dam[...])
            parent_hot[pl.ds(pl.multiple_of(i * 128, 128), 128), :] = here.astype(F32).astype(BF16)
            return carry

        lax.fori_loop(0, OWN * SLOTS // 128, some, 0)

    def pedigree_out(op, value):
        relay_out(0, op, dot(halves(value), send_hot[...]))

    def pedigree_mid(op, value):
        parents = fold(dot(relay_in(0, op), parent_hot[...]))
        term = mend[...] * (value - 0.5 * parents)
        back = -0.5 * fold(dot_nt(halves(term), parent_hot[...]))
        high = back.astype(BF16).astype(F32)
        relay_out(1, op, jnp.concatenate([high, back - high], axis=0))
        return term

    def pedigree_end(op, term):
        return term + fold(dot_nt(relay_in(1, op), send_hot[...]))

    def share_field(value):
        field[1, mine, :] = value.astype(BF16)

        def give(k, carry):
            piece = field.at[1, mine, :]
            remote(piece, piece, x_s, x_r, at_s(k)).start()
            return carry

        lax.fori_loop(1, S, give, 0)

    def field_arrives():
        settle(field.at[1, 0 : COLS - SHARE, :], x_s, x_r, at_s(1)).wait_recv()

    def dots_out(batch, one, two):
        tile = jnp.where(
            lane == 0,
            jnp.sum(one, axis=1, keepdims=True),
            jnp.where(lane == 1, jnp.sum(two, axis=1, keepdims=True), 0.0),
        )
        dot_send[batch] = tile

        def give(k, carry):
            remote(
                dot_send.at[batch], dot_recv.at[batch, a], d_s.at[batch], d_r.at[batch], at_a(k)
            ).start()
            return carry

        lax.fori_loop(1, OWN, give, 0)

    def dots_in(batch):
        settle(dot_recv.at[batch, 0 : OWN - 1], d_s.at[batch], d_r.at[batch], at_a(1)).wait_recv()
        dot_recv[batch, a] = dot_send[batch]
        total = jnp.sum(dot_recv[batch], axis=0)
        return total[:, 0:1], total[:, 1:2]

    effects_out(0)
    make_send_hot()
    pedigree_out(0, b_share)
    make_parent_hot()
    effects_mid(0)
    term = pedigree_mid(0, b_share)
    effects_sum(0)
    effects_spread(0)
    genomic_own(0)
    ped = pedigree_end(0, term)
    w_share = d_share * b_share + ped + scale * genomic(0)
    share_field(w_share)
    dots_out(0, b_share * b_share, w_share * b_share)
    pedigree_out(1, w_share)
    field_arrives()

    effects_out(1)
    gamma0, delta0 = dots_in(0)
    alpha0 = gamma0 / delta0
    r_share = b_share - alpha0 * w_share
    dots_out(1, r_share * r_share, r_share * w_share)
    term = pedigree_mid(1, w_share)
    effects_mid(1)
    effects_sum(1)
    effects_spread(1)
    genomic_own(1)
    ped = pedigree_end(1, term)
    gamma1, _ = dots_in(1)
    q_share = d_share * w_share + ped + scale * genomic(1)
    w1_share = w_share - alpha0 * q_share
    dots_out(2, w1_share * r_share, w1_share)
    delta1, _ = dots_in(2)
    beta = gamma1 / gamma0
    alpha1 = gamma1 / (delta1 - beta * gamma1 / alpha0)
    final[0, mine, :] = alpha0 * b_share + alpha1 * (r_share + beta * b_share)
    final[1, mine, :] = r_share - alpha1 * (w1_share + beta * w_share)

    def give(k, carry):
        piece = final.at[:, mine, :]
        remote(piece, piece, f_s, f_r, at_s(k)).start()
        return carry

    lax.fori_loop(1, S, give, 0)
    settle(final.at[:, 0 : COLS - SHARE, :], f_s, f_r, at_s(1)).wait()
    x_out[...] = final[0]
    r_out[...] = final[1]

    for op in range(2):
        for sub in range(SUBS):
            here = slice(sub * SUB, (sub + 1) * SUB)
            for k in range(1, Y):
                settle(
                    y_send.at[op, 0, :, here], y_s.at[op, k - 1, sub], y_r.at[op, 0, sub], at_y(k)
                ).wait_send()
                settle(
                    effects.at[op, :, y_lanes(y, sub)],
                    yg_s.at[op, k - 1, sub], yg_r.at[op, 0, sub], at_y(k),
                ).wait_send()
            settle(
                z_send.at[op, 0 : COLS - ZSHARE, here], z_s.at[op, sub], z_r.at[op, sub], at_z(1)
            ).wait_send()
            settle(
                effects.at[op, 0 : COLS - ZSHARE, y_lanes(y, sub)],
                zg_s.at[op, sub], zg_r.at[op, sub], at_z(1),
            ).wait_send()
        settle(g_send.at[op, 0 : COLS - SHARE, :], g_s.at[op], g_r.at[op], at_s(1)).wait_send()
        for leg in range(2):
            settle(
                p_recv.at[op, leg, 0 : OWN - 1], p_s.at[op, leg], p_r.at[op, leg], at_a(1)
            ).wait_send()
    settle(field.at[1, 0 : COLS - SHARE, :], x_s, x_r, at_s(1)).wait_send()
    for batch in range(3):
        settle(
            dot_recv.at[batch, 0 : OWN - 1], d_s.at[batch], d_r.at[batch], at_a(1)
        ).wait_send()


def local(geno, freq, rhs, diag, mend, weight, send_rows, sire, dam):
    vmem = pl.BlockSpec(memory_space=pltpu.VMEM)
    dma = pltpu.SemaphoreType.DMA
    x_t, r_t = pl.pallas_call(
        kernel,
        out_shape=(jax.ShapeDtypeStruct((COLS, ROWS), F32),) * 2,
        in_specs=[pl.BlockSpec(memory_space=pl.ANY)] + [vmem] * 8,
        out_specs=(vmem, vmem),
        scratch_shapes=[
            pltpu.VMEM((ROWS, LOCAL), BF16),
            pltpu.VMEM((ROWS, OWN * SLOTS), BF16),
            pltpu.VMEM((OWN * SLOTS, ROWS), BF16),
            pltpu.VMEM((2, COLS, ROWS), BF16),
            pltpu.VMEM((COLS, ROWS), F32),
            pltpu.VMEM((COLS, ROWS), F32),
            pltpu.VMEM((COLS, YCH), F32),
            pltpu.VMEM((2, Y, COLS, YCH), BF16),
            pltpu.VMEM((2, Y, COLS, YCH), BF16),
            pltpu.VMEM((COLS, YCH), F32),
            pltpu.VMEM((2, COLS, YCH), BF16),
            pltpu.VMEM((2, Z, ZSHARE, YCH), BF16),
            pltpu.VMEM((2, COLS, LOCAL), BF16),
            pltpu.VMEM((COLS, ROWS), F32),
            pltpu.VMEM((2, COLS, ROWS), BF16),
            pltpu.VMEM((2, S, SHARE, ROWS), BF16),
            pltpu.VMEM((2, 2, OWN, SHARE, 2 * SLOTS), BF16),
            pltpu.VMEM((2, 2, OWN, SHARE, 2 * SLOTS), BF16),
            pltpu.VMEM((2 * SHARE, OWN * SLOTS), BF16),
            pltpu.VMEM((3, SHARE, 128), F32),
            pltpu.VMEM((3, OWN, SHARE, 128), F32),
            pltpu.VMEM((2, COLS, ROWS), F32),
            dma((Y,)),
            dma((2, Y - 1, SUBS)), dma((2, Y, SUBS)),
            dma((2, SUBS)), dma((2, SUBS)),
            dma((2, SUBS)), dma((2, SUBS)),
            dma((2, Y - 1, SUBS)), dma((2, Y, SUBS)),
            dma((2,)), dma((2,)),
            dma, dma,
            dma((2, 2)), dma((2, 2)),
            dma((3,)), dma((3,)),
            dma, dma,
        ],
        compiler_params=pltpu.CompilerParams(
            collective_id=0, has_side_effects=True, vmem_limit_bytes=56 * 2**20
        ),
        cost_estimate=pl.CostEstimate(
            flops=5_000_000_000, bytes_accessed=12_000_000, transcendentals=0
        ),
    )(
        geno,
        freq.reshape(1, LOCAL),
        rhs,
        diag,
        mend.reshape(1, ROWS),
        weight.reshape(COLS, 1),
        send_rows[0],
        sire.reshape(1, ROWS),
        dam.reshape(1, ROWS),
    )
    return x_t.T, r_t.T


def solution(mesh):
    placed = (
        P("animal", "snp"),
        P("snp"),
        P("animal", None),
        P("animal", None),
        P("animal"),
        P(),
        P("animal", None, None),
        P("animal"),
        P("animal"),
    )
    return jax.shard_map(
        local,
        mesh=mesh,
        in_specs=placed,
        out_specs=(P("animal", None), P("animal", None)),
        check_vma=False,
    )
```

```python
import functools

import jax
import jax.numpy as jnp
from jax import lax
from jax.experimental import pallas as pl
from jax.experimental.pallas import tpu as pltpu
from jax.sharding import PartitionSpec as P

MESH = pl.DeviceIdType.MESH
SNPS = 32768
Z, Y, S = 8, 4, 8
OWN = Z * Y
COLS, ROWS, LOCAL = 128, 1024, 4096
SHARE = COLS // S
ZSHARE = COLS // Z
YCH = LOCAL // Y
SUBS = 4
SUB = YCH // SUBS
SLOTS = 64
NT = (((1,), (1,)), ((), ()))
F32, BF16 = jnp.float32, jnp.bfloat16


def dot(a, b):
    return jnp.dot(a, b, preferred_element_type=F32)


def dot_nt(a, b):
    return lax.dot_general(a, b, NT, preferred_element_type=F32)


def halves(value):
    high = value.astype(BF16)
    low = (value - high.astype(F32)).astype(BF16)
    return jnp.concatenate([high, low], axis=0)


def swap(value):
    return pltpu.roll(value, SLOTS, 1)


def kernel(
    geno, freq, rhs, diag, mend, weight, rows, sire, dam,
    x_out, r_out,
    block, send_hot, parent_hot, field, field_t, diag_t,
    y_own, y_send, y_recv, z_own, z_send, z_recv, effects,
    g_own, g_send, g_recv, p_send, p_recv, p_mat, dot_send, dot_recv,
    w_full, result, scalars, norm, norm_send, norm_recv,
    load_sem, y_s, y_r, z_s, z_r, zg_s, zg_r, yg_s, yg_r, g_s, g_r, x_s, x_r,
    p_s, p_r, d_s, d_r, w_s, w_r, c_s, c_r, f_s, f_r, n_s, n_r,
):
    a, s = lax.axis_index("animal"), lax.axis_index("snp")
    z, y = a // Y, a % Y

    def at_y(k):
        return (z * Y + (y + k) % Y, s)

    def at_z(k):
        return (((z + k) % Z) * Y + y, s)

    def at_s(k):
        return (a, (s + k) % S)

    def at_a(k):
        return ((a + k) % OWN, s)

    def remote(src, dst, send_sem, recv_sem, peer):
        return pltpu.make_async_remote_copy(
            src_ref=src, dst_ref=dst, send_sem=send_sem, recv_sem=recv_sem,
            device_id=peer, device_id_type=MESH,
        )

    def settle(ref, send_sem, recv_sem, peer):
        return remote(ref, ref, send_sem, recv_sem, peer)

    def y_lanes(which, sub):
        return pl.ds(pl.multiple_of(which * YCH + sub * SUB, SUB), SUB)

    def loads(which, sub):
        lanes = y_lanes(which, sub)
        return pltpu.make_async_copy(
            geno.at[:, lanes], block.at[:, lanes], load_sem.at[which, sub]
        )

    for sub in range(SUBS):
        for k in range(1, Y + 1):
            loads((y + k) % Y, sub).start()

    barrier = pltpu.get_barrier_semaphore()

    def greet_a(k, carry):
        pl.semaphore_signal(barrier, inc=1, device_id=at_a(k), device_id_type=MESH)
        return carry

    def greet_s(k, carry):
        pl.semaphore_signal(barrier, inc=1, device_id=at_s(k), device_id_type=MESH)
        return carry

    lax.fori_loop(1, OWN, greet_a, 0)
    lax.fori_loop(1, S, greet_s, 0)

    field_t[...] = rhs[...].T
    diag_t[...] = diag[...].T
    field[0] = field_t[...].astype(BF16)
    mine = pl.ds(pl.multiple_of(s * SHARE, SHARE), SHARE)
    z_mine = pl.ds(pl.multiple_of(z * ZSHARE, ZSHARE), ZSHARE)
    b_share = field_t[mine, :]
    d_share = diag_t[mine, :]
    lane = lax.broadcasted_iota(jnp.int32, (SHARE, 2 * SLOTS), 1)
    place = lax.broadcasted_iota(jnp.int32, (SHARE, COLS), 0) + s * SHARE
    scale = jnp.sum(
        jnp.where(lane == place, weight[...], 0.0), axis=1, keepdims=True
    ) * (1.0 / SNPS)
    first = lane < SLOTS

    pl.semaphore_wait(barrier, OWN - 1 + S - 1)

    def centre(which, sub):
        loads(which, sub).wait()
        lanes = y_lanes(which, sub)
        twice = 2.0 * freq[:, lanes]

        def rows_of(i, carry):
            at = pl.ds(pl.multiple_of(i * 256, 256), 256)
            block[at, lanes] = (block[at, lanes].astype(F32) - twice).astype(BF16)
            return carry

        lax.fori_loop(0, ROWS // 256, rows_of, 0)

    def spot(sub):
        return slice(sub * SUB, (sub + 1) * SUB)

    def effects_out(op, sub):
        here = spot(sub)

        def one(k, carry):
            which = (y + k) % Y
            if op == 0:
                centre(which, sub)
            value = dot(field[op], block[:, y_lanes(which, sub)])
            y_send[op, which, :, here] = value.astype(BF16)
            remote(
                y_send.at[op, which, :, here], y_recv.at[op, y, :, here],
                y_s.at[op, k - 1, sub], y_r.at[op, y, sub], at_y(k),
            ).start()
            return carry

        lax.fori_loop(1, Y, one, 0)
        if op == 0:
            centre(y, sub)
        y_own[:, here] = dot(field[op], block[:, y_lanes(y, sub)])

    def effects_mid(op, sub):
        here = spot(sub)
        total = y_own[:, here]
        for k in range(1, Y):
            which = (y + k) % Y
            piece = y_recv.at[op, which, :, here]
            settle(piece, y_s.at[op, k - 1, sub], y_r.at[op, which, sub], at_y(k)).wait_recv()
            total = total + piece[...].astype(F32)
        z_own[:, here] = total
        z_send[op, :, here] = total.astype(BF16)

        def give(k, carry):
            peer_rows = pl.ds(pl.multiple_of(((z + k) % Z) * ZSHARE, ZSHARE), ZSHARE)
            remote(
                z_send.at[op, peer_rows, here], z_recv.at[op, z, :, here],
                z_s.at[op, sub], z_r.at[op, sub], at_z(k),
            ).start()
            return carry

        lax.fori_loop(1, Z, give, 0)

    def effects_sum(op, sub):
        here = spot(sub)
        settle(
            z_recv.at[op, 0 : Z - 1, :, here], z_s.at[op, sub], z_r.at[op, sub], at_z(1)
        ).wait_recv()
        total = z_own[z_mine, here]
        for k in range(1, Z):
            total = total + z_recv[op, (z + k) % Z, :, here].astype(F32)
        effects[op, z_mine, y_lanes(y, sub)] = total.astype(BF16)

        def give(k, carry):
            piece = effects.at[op, z_mine, y_lanes(y, sub)]
            remote(piece, piece, zg_s.at[op, sub], zg_r.at[op, sub], at_z(k)).start()
            return carry

        lax.fori_loop(1, Z, give, 0)

    def take(op, lanes, fresh):
        piece = effects[op, :, lanes]
        value = dot_nt(piece, block[:, lanes])
        if fresh:
            g_own[...] = value
        else:
            g_own[...] += value
        if op == 1:
            wide = piece.astype(F32)
            square = jnp.zeros((COLS, 128), F32)
            for part in range(SUB // 128):
                one = wide[:, part * 128 : (part + 1) * 128]
                square = square + one * one
            if fresh:
                norm[...] = square
            else:
                norm[...] += square

    def effects_spread(op, sub):
        lanes = y_lanes(y, sub)
        settle(
            effects.at[op, 0 : COLS - ZSHARE, lanes], zg_s.at[op, sub], zg_r.at[op, sub], at_z(1)
        ).wait_recv()
        for k in range(1, Y):
            piece = effects.at[op, :, lanes]
            remote(piece, piece, yg_s.at[op, k - 1, sub], yg_r.at[op, y, sub], at_y(k)).start()
        take(op, lanes, sub == 0)

    def genomic(op):
        for sub in range(SUBS):
            def one(k, carry):
                which = (y + k) % Y
                lanes = y_lanes(which, sub)
                settle(
                    effects.at[op, :, lanes],
                    yg_s.at[op, k - 1, sub], yg_r.at[op, which, sub], at_y(k),
                ).wait_recv()
                take(op, lanes, False)
                return carry

            lax.fori_loop(1, Y, one, 0)
        g_send[op] = g_own[...].astype(BF16)
        if op == 1:
            norm_send[...] = jnp.broadcast_to(
                jnp.sum(norm[...], axis=1, keepdims=True), (COLS, 128)
            )

        def give(k, carry):
            peer_rows = pl.ds(pl.multiple_of(((s + k) % S) * SHARE, SHARE), SHARE)
            if op == 1:
                remote(norm_send.at[peer_rows, :], norm_recv.at[s], n_s, n_r, at_s(k)).start()
            remote(
                g_send.at[op, peer_rows, :], g_recv.at[op, s], g_s.at[op], g_r.at[op], at_s(k)
            ).start()
            return carry

        lax.fori_loop(1, S, give, 0)

    def genomic_in(op):
        settle(g_recv.at[op, 0 : S - 1], g_s.at[op], g_r.at[op], at_s(1)).wait_recv()
        total = g_own[mine, :]
        for k in range(1, S):
            total = total + g_recv[op, (s + k) % S].astype(F32)
        return total

    def norm_in():
        settle(norm_recv.at[0 : S - 1], n_s, n_r, at_s(1)).wait_recv()
        total = norm_send[mine, :]
        for k in range(1, S):
            total = total + norm_recv[(s + k) % S]
        return total[:, 0:1]

    def relay_out(leg, op, value):
        both = value
        for pair in range(OWN // 2):
            lanes = slice(pair * 2 * SLOTS, (pair + 1) * 2 * SLOTS)
            high, low = both[:SHARE, lanes], both[SHARE:, lanes]
            p_send[op, leg, 2 * pair] = jnp.where(first, high, swap(low)).astype(BF16)
            p_send[op, leg, 2 * pair + 1] = jnp.where(first, swap(high), low).astype(BF16)

        def give(k, carry):
            peer = (a + k) % OWN
            remote(
                p_send.at[op, leg, peer], p_recv.at[op, leg, a],
                p_s.at[op, leg], p_r.at[op, leg], at_a(k),
            ).start()
            return carry

        lax.fori_loop(1, OWN, give, 0)

    def relay_in(leg, op):
        settle(
            p_recv.at[op, leg, 0 : OWN - 1], p_s.at[op, leg], p_r.at[op, leg], at_a(1)
        ).wait_recv()
        p_recv[op, leg, a] = p_send[op, leg, a]
        for pair in range(OWN // 2):
            lanes = slice(pair * 2 * SLOTS, (pair + 1) * 2 * SLOTS)
            one = p_recv[op, leg, 2 * pair].astype(F32)
            two = p_recv[op, leg, 2 * pair + 1].astype(F32)
            p_mat[:SHARE, lanes] = jnp.where(first, one, swap(two)).astype(BF16)
            p_mat[SHARE:, lanes] = jnp.where(first, swap(one), two).astype(BF16)
        return p_mat[...]

    def fold(both):
        return both[:SHARE] + both[SHARE:]

    def make_send_hot():
        even = rows[pl.ds(0, OWN // 2, stride=2), :]
        odd = rows[pl.ds(1, OWN // 2, stride=2), :]
        pairs = jnp.concatenate([even, odd], axis=1)
        at = lax.broadcasted_iota(jnp.int32, (ROWS, 2 * SLOTS), 0)
        for pair in range(OWN // 2):
            lanes = slice(pair * 2 * SLOTS, (pair + 1) * 2 * SLOTS)
            send_hot[:, lanes] = (at == pairs[pair : pair + 1, :]).astype(F32).astype(BF16)

    def make_parent_hot():
        def some(i, carry):
            at = lax.broadcasted_iota(jnp.int32, (128, ROWS), 0) + i * 128
            here = (at == sire[...]) | (at == dam[...])
            parent_hot[pl.ds(pl.multiple_of(i * 128, 128), 128), :] = here.astype(F32).astype(BF16)
            return carry

        lax.fori_loop(0, OWN * SLOTS // 128, some, 0)

    def pedigree_out(op, value):
        relay_out(0, op, dot(halves(value), send_hot[...]))

    def pedigree_mid(op, value):
        parents = fold(dot(relay_in(0, op), parent_hot[...]))
        term = mend[...] * (value - 0.5 * parents)
        form = term * (value - 0.5 * parents)
        back = -0.5 * fold(dot_nt(halves(term), parent_hot[...]))
        high = back.astype(BF16).astype(F32)
        relay_out(1, op, jnp.concatenate([high, back - high], axis=0))
        return term, form

    def pedigree_end(op, term):
        return term + fold(dot_nt(relay_in(1, op), send_hot[...]))

    def share_field(value):
        field[1, mine, :] = value.astype(BF16)

        def give(k, carry):
            piece = field.at[1, mine, :]
            remote(piece, piece, x_s, x_r, at_s(k)).start()
            return carry

        lax.fori_loop(1, S, give, 0)

    def field_arrives():
        settle(field.at[1, 0 : COLS - SHARE, :], x_s, x_r, at_s(1)).wait_recv()

    def pack(*columns):
        tile = jnp.zeros((SHARE, 128), F32)
        for position, column in enumerate(columns):
            tile = jnp.where(lane == position, column, tile)
        return tile

    def dots_out(batch, *products):
        dot_send[batch] = pack(*[jnp.sum(p, axis=1, keepdims=True) for p in products])

        def give(k, carry):
            remote(
                dot_send.at[batch], dot_recv.at[batch, a], d_s.at[batch], d_r.at[batch], at_a(k)
            ).start()
            return carry

        lax.fori_loop(1, OWN, give, 0)

    def dots_in(batch):
        settle(dot_recv.at[batch, 0 : OWN - 1], d_s.at[batch], d_r.at[batch], at_a(1)).wait_recv()
        dot_recv[batch, a] = dot_send[batch]
        total = jnp.sum(dot_recv[batch], axis=0)
        return total[:, 0:1], total[:, 1:2], total[:, 2:3]

    def to_snp(ref, send_sem, recv_sem):
        def give(k, carry):
            piece = ref.at[mine, :]
            remote(piece, piece, send_sem, recv_sem, at_s(k)).start()
            return carry

        lax.fori_loop(1, S, give, 0)

    def all_of(ref, send_sem, recv_sem):
        return settle(ref.at[0 : COLS - SHARE, :], send_sem, recv_sem, at_s(1))

    effects_out(0, 0)
    effects_out(0, 1)
    effects_out(0, 2)
    effects_mid(0, 0)
    effects_out(0, 3)
    effects_mid(0, 1)
    make_send_hot()
    pedigree_out(0, b_share)
    effects_mid(0, 2)
    effects_sum(0, 0)
    effects_mid(0, 3)
    effects_sum(0, 1)
    make_parent_hot()
    effects_sum(0, 2)
    effects_spread(0, 0)
    effects_sum(0, 3)
    effects_spread(0, 1)
    term, _ = pedigree_mid(0, b_share)
    effects_spread(0, 2)
    effects_spread(0, 3)
    ped = pedigree_end(0, term)
    genomic(0)
    w_share = d_share * b_share + ped + scale * genomic_in(0)
    share_field(w_share)
    pedigree_out(1, w_share)
    dots_out(0, b_share * b_share, w_share * b_share, w_share * w_share)
    w_full[mine, :] = w_share
    field_arrives()

    effects_out(1, 0)
    effects_out(1, 1)
    to_snp(w_full, w_s, w_r)
    effects_out(1, 2)
    effects_mid(1, 0)
    effects_out(1, 3)
    effects_mid(1, 1)
    term, form = pedigree_mid(1, w_share)
    effects_mid(1, 2)
    effects_sum(1, 0)
    effects_mid(1, 3)
    effects_sum(1, 1)
    gamma0, delta0, square0 = dots_in(0)
    alpha0 = gamma0 / delta0
    r_share = b_share - alpha0 * w_share
    dots_out(1, r_share * r_share, r_share * w_share, d_share * w_share * w_share + form)
    effects_sum(1, 2)
    effects_spread(1, 0)
    effects_sum(1, 3)
    effects_spread(1, 1)
    effects_spread(1, 2)
    effects_spread(1, 3)
    ped = pedigree_end(1, term)
    gamma1, cross, quad = dots_in(1)
    beta = gamma1 / gamma0
    genomic(1)
    quad = quad + scale * norm_in()
    delta1 = cross - alpha0 * (square0 - alpha0 * quad)
    alpha1 = gamma1 / (delta1 - beta * gamma1 / alpha0)
    scalars[mine, :] = pack(alpha0, beta, alpha1)
    to_snp(scalars, c_s, c_r)
    q_share = d_share * w_share + ped + scale * genomic_in(1)
    w1_share = w_share - alpha0 * q_share
    result[mine, :] = (r_share - alpha1 * (w1_share + beta * w_share)).astype(BF16)
    to_snp(result, f_s, f_r)
    all_of(w_full, w_s, w_r).wait()
    all_of(scalars, c_s, c_r).wait()
    alpha0, beta, alpha1 = (scalars[:, i : i + 1] for i in range(3))
    b_full = field_t[...]
    x_out[...] = (
        alpha0 * b_full + alpha1 * ((b_full - alpha0 * w_full[...]) + beta * b_full)
    ).T
    all_of(result, f_s, f_r).wait()
    r_out[...] = result[...].astype(F32).T

    for op in range(2):
        for sub in range(SUBS):
            here = spot(sub)
            for k in range(1, Y):
                settle(
                    y_send.at[op, 0, :, here], y_s.at[op, k - 1, sub], y_r.at[op, 0, sub], at_y(k)
                ).wait_send()
                settle(
                    effects.at[op, :, y_lanes(y, sub)],
                    yg_s.at[op, k - 1, sub], yg_r.at[op, 0, sub], at_y(k),
                ).wait_send()
            settle(
                z_send.at[op, 0 : COLS - ZSHARE, here], z_s.at[op, sub], z_r.at[op, sub], at_z(1)
            ).wait_send()
            settle(
                effects.at[op, 0 : COLS - ZSHARE, y_lanes(y, sub)],
                zg_s.at[op, sub], zg_r.at[op, sub], at_z(1),
            ).wait_send()
        settle(g_send.at[op, 0 : COLS - SHARE, :], g_s.at[op], g_r.at[op], at_s(1)).wait_send()
        for leg in range(2):
            settle(
                p_recv.at[op, leg, 0 : OWN - 1], p_s.at[op, leg], p_r.at[op, leg], at_a(1)
            ).wait_send()
    settle(field.at[1, 0 : COLS - SHARE, :], x_s, x_r, at_s(1)).wait_send()
    settle(norm_recv.at[0 : S - 1], n_s, n_r, at_s(1)).wait_send()
    for batch in range(2):
        settle(
            dot_recv.at[batch, 0 : OWN - 1], d_s.at[batch], d_r.at[batch], at_a(1)
        ).wait_send()


def local(geno, freq, rhs, diag, mend, weight, send_rows, sire, dam):
    vmem = pl.BlockSpec(memory_space=pltpu.VMEM)
    dma = pltpu.SemaphoreType.DMA
    return pl.pallas_call(
        kernel,
        out_shape=(jax.ShapeDtypeStruct((ROWS, COLS), F32),) * 2,
        in_specs=[pl.BlockSpec(memory_space=pl.ANY)] + [vmem] * 8,
        out_specs=(vmem, vmem),
        scratch_shapes=[
            pltpu.VMEM((ROWS, LOCAL), BF16),
            pltpu.VMEM((ROWS, OWN * SLOTS), BF16),
            pltpu.VMEM((OWN * SLOTS, ROWS), BF16),
            pltpu.VMEM((2, COLS, ROWS), BF16),
            pltpu.VMEM((COLS, ROWS), F32),
            pltpu.VMEM((COLS, ROWS), F32),
            pltpu.VMEM((COLS, YCH), F32),
            pltpu.VMEM((2, Y, COLS, YCH), BF16),
            pltpu.VMEM((2, Y, COLS, YCH), BF16),
            pltpu.VMEM((COLS, YCH), F32),
            pltpu.VMEM((2, COLS, YCH), BF16),
            pltpu.VMEM((2, Z, ZSHARE, YCH), BF16),
            pltpu.VMEM((2, COLS, LOCAL), BF16),
            pltpu.VMEM((COLS, ROWS), F32),
            pltpu.VMEM((2, COLS, ROWS), BF16),
            pltpu.VMEM((2, S, SHARE, ROWS), BF16),
            pltpu.VMEM((2, 2, OWN, SHARE, 2 * SLOTS), BF16),
            pltpu.VMEM((2, 2, OWN, SHARE, 2 * SLOTS), BF16),
            pltpu.VMEM((2 * SHARE, OWN * SLOTS), BF16),
            pltpu.VMEM((2, SHARE, 128), F32),
            pltpu.VMEM((2, OWN, SHARE, 128), F32),
            pltpu.VMEM((COLS, ROWS), F32),
            pltpu.VMEM((COLS, ROWS), BF16),
            pltpu.VMEM((COLS, 128), F32),
            pltpu.VMEM((COLS, 128), F32),
            pltpu.VMEM((COLS, 128), F32),
            pltpu.VMEM((S, SHARE, 128), F32),
            dma((Y, SUBS)),
            dma((2, Y - 1, SUBS)), dma((2, Y, SUBS)),
            dma((2, SUBS)), dma((2, SUBS)),
            dma((2, SUBS)), dma((2, SUBS)),
            dma((2, Y - 1, SUBS)), dma((2, Y, SUBS)),
            dma((2,)), dma((2,)),
            dma, dma,
            dma((2, 2)), dma((2, 2)),
            dma((2,)), dma((2,)),
            dma, dma,
            dma, dma,
            dma, dma,
            dma, dma,
        ],
        compiler_params=pltpu.CompilerParams(
            collective_id=0, has_side_effects=True, vmem_limit_bytes=56 * 2**20
        ),
        cost_estimate=pl.CostEstimate(
            flops=5_000_000_000, bytes_accessed=12_000_000, transcendentals=0
        ),
    )(
        geno,
        freq.reshape(1, LOCAL),
        rhs,
        diag,
        mend.reshape(1, ROWS),
        weight.reshape(1, COLS),
        send_rows[0],
        sire.reshape(1, ROWS),
        dam.reshape(1, ROWS),
    )


def solution(mesh):
    placed = (
        P("animal", "snp"),
        P("snp"),
        P("animal", None),
        P("animal", None),
        P("animal"),
        P(),
        P("animal", None, None),
        P("animal"),
        P("animal"),
    )
    return jax.shard_map(
        local,
        mesh=mesh,
        in_specs=placed,
        out_specs=(P("animal", None), P("animal", None)),
        check_vma=False,
    )
```

```python
import functools

import jax
import jax.numpy as jnp
from jax import lax
from jax.experimental import pallas as pl
from jax.experimental.pallas import tpu as pltpu
from jax.sharding import PartitionSpec as P

MESH = pl.DeviceIdType.MESH
SNPS = 32768
Z, Y, S = 8, 4, 8
OWN = Z * Y
COLS, ROWS, LOCAL = 128, 1024, 4096
SHARE = COLS // S
ZSHARE = COLS // Z
YCH = LOCAL // Y
SUBS = 4
SUB = YCH // SUBS
SLOTS = 64
PARTS = 3
NT = (((1,), (1,)), ((), ()))
F32, BF16 = jnp.float32, jnp.bfloat16


def dot(a, b):
    return jnp.dot(a, b, preferred_element_type=F32)


def dot_nt(a, b):
    return lax.dot_general(a, b, NT, preferred_element_type=F32)


def halves(value):
    high = value.astype(BF16)
    low = (value - high.astype(F32)).astype(BF16)
    return jnp.concatenate([high, low], axis=0)


def swap(value):
    return pltpu.roll(value, SLOTS, 1)


def kernel(
    geno, freq, rhs, diag, mend, weight, rows, sire, dam,
    x_out, r_out,
    block, send_hot, parent_hot, field, field_t, diag_t,
    y_own, y_send, y_recv, z_own, z_send, z_recv, effects,
    g_own, g_send, g_recv, p_send, p_recv, p_mat,
    w_full, result, scalars, norm, norm_send, norm_recv,
    load_sem, y_s, y_r, z_s, z_r, zg_s, zg_r, yg_s, yg_r, g_s, g_r, x_s, x_r,
    p_s, p_r, w_s, w_r, c_s, c_r, f_s, f_r, n_s, n_r,
):
    a, s = lax.axis_index("animal"), lax.axis_index("snp")
    z, y = a // Y, a % Y

    def at_y(k):
        return (z * Y + (y + k) % Y, s)

    def at_z(k):
        return (((z + k) % Z) * Y + y, s)

    def at_s(k):
        return (a, (s + k) % S)

    def at_a(k):
        return ((a + k) % OWN, s)

    def remote(src, dst, send_sem, recv_sem, peer):
        return pltpu.make_async_remote_copy(
            src_ref=src, dst_ref=dst, send_sem=send_sem, recv_sem=recv_sem,
            device_id=peer, device_id_type=MESH,
        )

    def settle(ref, send_sem, recv_sem, peer):
        return remote(ref, ref, send_sem, recv_sem, peer)

    def y_lanes(which, sub):
        return pl.ds(pl.multiple_of(sub * YCH + which * SUB, SUB), SUB)

    def chunk(sub):
        return slice(sub * YCH, (sub + 1) * YCH)

    def loads(sub):
        return pltpu.make_async_copy(
            geno.at[:, chunk(sub)], block.at[:, chunk(sub)], load_sem.at[sub]
        )

    for sub in range(SUBS):
        loads(sub).start()

    barrier = pltpu.get_barrier_semaphore()

    def greet_a(k, carry):
        pl.semaphore_signal(barrier, inc=1, device_id=at_a(k), device_id_type=MESH)
        return carry

    def greet_s(k, carry):
        pl.semaphore_signal(barrier, inc=1, device_id=at_s(k), device_id_type=MESH)
        return carry

    lax.fori_loop(1, OWN, greet_a, 0)
    lax.fori_loop(1, S, greet_s, 0)

    field_t[...] = rhs[...].T
    field[0] = field_t[...].astype(BF16)
    mine = pl.ds(pl.multiple_of(s * SHARE, SHARE), SHARE)
    z_mine = pl.ds(pl.multiple_of(z * ZSHARE, ZSHARE), ZSHARE)
    b_share = field_t[mine, :]
    lane = lax.broadcasted_iota(jnp.int32, (SHARE, 2 * SLOTS), 1)
    place = lax.broadcasted_iota(jnp.int32, (SHARE, COLS), 0) + s * SHARE
    scale = jnp.sum(
        jnp.where(lane == place, weight[...], 0.0), axis=1, keepdims=True
    ) * (1.0 / SNPS)
    first = lane < SLOTS

    def centre(sub):
        loads(sub).wait()
        lanes = chunk(sub)
        twice = 2.0 * freq[:, lanes]

        def rows_of(i, carry):
            at = pl.ds(pl.multiple_of(i * 128, 128), 128)
            block[at, lanes] = (block[at, lanes].astype(F32) - twice).astype(BF16)
            return carry

        lax.fori_loop(0, ROWS // 128, rows_of, 0)

    def spot(sub):
        return slice(sub * SUB, (sub + 1) * SUB)

    def effects_send(op, sub):
        for k in range(1, Y):
            remote(
                y_send.at[op, :, y_lanes((y + k) % Y, sub)], y_recv.at[op, y, :, spot(sub)],
                y_s.at[op, k - 1, sub], y_r.at[op, y, sub], at_y(k),
            ).start()

    def effects_out(op, sub, send=True):
        if op == 0:
            centre(sub)
        value = dot(field[op], block[:, chunk(sub)])
        y_send[op, :, chunk(sub)] = value.astype(BF16)
        if send:
            effects_send(op, sub)
        y_own[:, chunk(sub)] = value

    def effects_mid(op, sub):
        here = spot(sub)
        total = y_own[:, y_lanes(y, sub)]
        for k in range(1, Y):
            which = (y + k) % Y
            piece = y_recv.at[op, which, :, here]
            settle(piece, y_s.at[op, k - 1, sub], y_r.at[op, which, sub], at_y(k)).wait_recv()
            total = total + piece[...].astype(F32)
        z_own[:, here] = total
        z_send[op, :, here] = total.astype(BF16)

        def give(k, carry):
            peer_rows = pl.ds(pl.multiple_of(((z + k) % Z) * ZSHARE, ZSHARE), ZSHARE)
            remote(
                z_send.at[op, peer_rows, here], z_recv.at[op, z, :, here],
                z_s.at[op, sub], z_r.at[op, sub], at_z(k),
            ).start()
            return carry

        lax.fori_loop(1, Z, give, 0)

    def effects_sum(op, sub):
        here = spot(sub)
        settle(
            z_recv.at[op, 0 : Z - 1, :, here], z_s.at[op, sub], z_r.at[op, sub], at_z(1)
        ).wait_recv()
        total = z_own[z_mine, here]
        for k in range(1, Z):
            total = total + z_recv[op, (z + k) % Z, :, here].astype(F32)
        effects[op, z_mine, y_lanes(y, sub)] = total.astype(BF16)

        def give(k, carry):
            piece = effects.at[op, z_mine, y_lanes(y, sub)]
            remote(piece, piece, zg_s.at[op, sub], zg_r.at[op, sub], at_z(k)).start()
            return carry

        lax.fori_loop(1, Z, give, 0)

    def effects_spread(op, sub):
        lanes = y_lanes(y, sub)
        settle(
            effects.at[op, 0 : COLS - ZSHARE, lanes], zg_s.at[op, sub], zg_r.at[op, sub], at_z(1)
        ).wait_recv()
        for k in range(1, Y):
            piece = effects.at[op, :, lanes]
            remote(piece, piece, yg_s.at[op, k - 1, sub], yg_r.at[op, y, sub], at_y(k)).start()

    def take(op, sub):
        for k in range(1, Y):
            which = (y + k) % Y
            settle(
                effects.at[op, :, y_lanes(which, sub)],
                yg_s.at[op, k - 1, sub], yg_r.at[op, which, sub], at_y(k),
            ).wait_recv()
        piece = effects[op, :, chunk(sub)]
        value = dot_nt(piece, block[:, chunk(sub)])
        if sub == 0:
            g_own[...] = value
        else:
            g_own[...] += value
        if op == 1:
            square = jnp.zeros((COLS, 128), F32)
            for part in range(YCH // 128):
                one = piece[:, part * 128 : (part + 1) * 128].astype(F32)
                square = square + one * one
            if sub == 0:
                norm[...] = square
            else:
                norm[...] += square

    def genomic_out(op):
        g_send[op] = g_own[...].astype(BF16)
        if op == 1:
            norm_send[...] = jnp.broadcast_to(
                jnp.sum(norm[...], axis=1, keepdims=True), (COLS, 128)
            )

        def give(k, carry):
            peer_rows = pl.ds(pl.multiple_of(((s + k) % S) * SHARE, SHARE), SHARE)
            if op == 1:
                remote(norm_send.at[peer_rows, :], norm_recv.at[s], n_s, n_r, at_s(k)).start()
            remote(
                g_send.at[op, peer_rows, :], g_recv.at[op, s], g_s.at[op], g_r.at[op], at_s(k)
            ).start()
            return carry

        lax.fori_loop(1, S, give, 0)

    def genomic_in(op):
        settle(g_recv.at[op, 0 : S - 1], g_s.at[op], g_r.at[op], at_s(1)).wait_recv()
        total = g_own[mine, :]
        for k in range(1, S):
            total = total + g_recv[op, (s + k) % S].astype(F32)
        return total

    def norm_in():
        settle(norm_recv.at[0 : S - 1], n_s, n_r, at_s(1)).wait_recv()
        total = norm_send[mine, :]
        for k in range(1, S):
            total = total + norm_recv[(s + k) % S]
        return total[:, 0:1]

    def pack(*columns):
        tile = jnp.zeros((SHARE, 128), F32)
        for position, column in enumerate(columns):
            tile = jnp.where(lane == position, column, tile)
        return tile

    def depth(op):
        return 2 * SHARE if op == 1 else SHARE

    def relay_out(leg, op, both, products=()):
        for pair in range(OWN // 2):
            lanes = slice(pair * 2 * SLOTS, (pair + 1) * 2 * SLOTS)
            high, low = both[:SHARE, lanes], both[SHARE:, lanes]
            p_send[op, leg, 2 * pair, :SHARE] = jnp.where(first, high, swap(low)).astype(BF16)
            p_send[op, leg, 2 * pair + 1, :SHARE] = jnp.where(first, swap(high), low).astype(BF16)
        if products:
            parts = []
            for product in products:
                left = jnp.sum(product, axis=1, keepdims=True)
                for _ in range(PARTS):
                    part = left.astype(BF16).astype(F32)
                    left = left - part
                    parts.append(part)
            tile = pack(*parts).astype(BF16)
            for peer in range(OWN):
                p_send[op, leg, peer, SHARE:] = tile

        def give(k, carry):
            peer = (a + k) % OWN
            remote(
                p_send.at[op, leg, peer, 0 : depth(op)], p_recv.at[op, leg, a, 0 : depth(op)],
                p_s.at[op, leg], p_r.at[op, leg], at_a(k),
            ).start()
            return carry

        lax.fori_loop(1, OWN, give, 0)

    def relay_in(leg, op):
        settle(
            p_recv.at[op, leg, 0 : OWN - 1, 0 : depth(op)],
            p_s.at[op, leg], p_r.at[op, leg], at_a(1),
        ).wait_recv()
        p_recv[op, leg, a] = p_send[op, leg, a]
        for pair in range(OWN // 2):
            lanes = slice(pair * 2 * SLOTS, (pair + 1) * 2 * SLOTS)
            one = p_recv[op, leg, 2 * pair, :SHARE].astype(F32)
            two = p_recv[op, leg, 2 * pair + 1, :SHARE].astype(F32)
            p_mat[:SHARE, lanes] = jnp.where(first, one, swap(two)).astype(BF16)
            p_mat[SHARE:, lanes] = jnp.where(first, swap(one), two).astype(BF16)
        return p_mat[...]

    def totals(leg):
        tile = jnp.sum(p_recv[1, leg, :, SHARE:, :].astype(F32), axis=0)
        return tuple(
            jnp.sum(tile[:, i * PARTS : (i + 1) * PARTS], axis=1, keepdims=True) for i in range(3)
        )

    def fold(both):
        return both[:SHARE] + both[SHARE:]

    def make_send_hot():
        even = rows[pl.ds(0, OWN // 2, stride=2), :]
        odd = rows[pl.ds(1, OWN // 2, stride=2), :]
        pairs = jnp.concatenate([even, odd], axis=1)
        at = lax.broadcasted_iota(jnp.int32, (ROWS, 2 * SLOTS), 0)
        for pair in range(OWN // 2):
            lanes = slice(pair * 2 * SLOTS, (pair + 1) * 2 * SLOTS)
            send_hot[:, lanes] = (at == pairs[pair : pair + 1, :]).astype(F32).astype(BF16)

    def make_parent_hot():
        def some(i, carry):
            at = lax.broadcasted_iota(jnp.int32, (128, ROWS), 0) + i * 128
            here = (at == sire[...]) | (at == dam[...])
            parent_hot[pl.ds(pl.multiple_of(i * 128, 128), 128), :] = here.astype(F32).astype(BF16)
            return carry

        lax.fori_loop(0, OWN * SLOTS // 128, some, 0)

    def pedigree_out(op, value, products=()):
        relay_out(0, op, dot(halves(value), send_hot[...]), products)

    def pedigree_mid(op, value):
        parents = fold(dot(relay_in(0, op), parent_hot[...]))
        lacks = value - 0.5 * parents
        return lacks, mend[...] * lacks

    def pedigree_back(op, value, lacks, term):
        back = -0.5 * fold(dot_nt(halves(term), parent_hot[...]))
        high = back.astype(BF16).astype(F32)
        both = jnp.concatenate([high, back - high], axis=0)
        if op == 0:
            relay_out(1, op, both)
            return ()
        gamma, delta, square = totals(0)
        alpha = gamma / delta
        rest = b_share - alpha * value
        relay_out(
            1, op, both, (rest * rest, rest * value, d_share * value * value + term * lacks)
        )
        return gamma, alpha, square, rest

    def pedigree_end(op, term):
        return term + fold(dot_nt(relay_in(1, op), send_hot[...]))

    def share_field(value):
        field[1, mine, :] = value.astype(BF16)

        def give(k, carry):
            piece = field.at[1, mine, :]
            remote(piece, piece, x_s, x_r, at_s(k)).start()
            return carry

        lax.fori_loop(1, S, give, 0)

    def field_arrives():
        settle(field.at[1, 0 : COLS - SHARE, :], x_s, x_r, at_s(1)).wait_recv()

    def to_snp(ref, send_sem, recv_sem):
        def give(k, carry):
            piece = ref.at[mine, :]
            remote(piece, piece, send_sem, recv_sem, at_s(k)).start()
            return carry

        lax.fori_loop(1, S, give, 0)

    def all_of(ref, send_sem, recv_sem):
        return settle(ref.at[0 : COLS - SHARE, :], send_sem, recv_sem, at_s(1))

    effects_out(0, 0, send=False)
    effects_out(0, 1, send=False)
    make_send_hot()
    pl.semaphore_wait(barrier, OWN - 1 + S - 1)
    effects_send(0, 0)
    effects_send(0, 1)
    effects_out(0, 2)
    effects_out(0, 3)
    pedigree_out(0, b_share)
    make_parent_hot()
    diag_t[...] = diag[...].T
    d_share = diag_t[mine, :]
    effects_mid(0, 0)
    effects_mid(0, 1)
    effects_mid(0, 2)
    effects_sum(0, 0)
    effects_mid(0, 3)
    effects_sum(0, 1)
    lacks, term = pedigree_mid(0, b_share)
    effects_spread(0, 0)
    pedigree_back(0, b_share, lacks, term)
    effects_sum(0, 2)
    effects_spread(0, 1)
    effects_sum(0, 3)
    effects_spread(0, 2)
    take(0, 0)
    effects_spread(0, 3)
    take(0, 1)
    take(0, 2)
    ped = pedigree_end(0, term)
    take(0, 3)
    genomic_out(0)
    w_share = d_share * b_share + ped
    w_share = w_share + scale * genomic_in(0)
    share_field(w_share)
    pedigree_out(1, w_share, (b_share * b_share, w_share * b_share, w_share * w_share))
    w_full[mine, :] = w_share
    field_arrives()

    effects_out(1, 0)
    effects_out(1, 1)
    effects_out(1, 2)
    effects_out(1, 3)
    to_snp(w_full, w_s, w_r)
    lacks, term = pedigree_mid(1, w_share)
    effects_mid(1, 0)
    gamma0, alpha0, square0, r_share = pedigree_back(1, w_share, lacks, term)
    effects_mid(1, 1)
    effects_mid(1, 2)
    effects_sum(1, 0)
    effects_mid(1, 3)
    effects_sum(1, 1)
    effects_spread(1, 0)
    effects_sum(1, 2)
    effects_spread(1, 1)
    effects_sum(1, 3)
    ped = pedigree_end(1, term)
    effects_spread(1, 2)
    take(1, 0)
    effects_spread(1, 3)
    take(1, 1)
    take(1, 2)
    gamma1, cross, quad = totals(1)
    beta = gamma1 / gamma0
    take(1, 3)
    genomic_out(1)
    quad = quad + scale * norm_in()
    delta1 = cross - alpha0 * (square0 - alpha0 * quad)
    alpha1 = gamma1 / (delta1 - beta * gamma1 / alpha0)
    scalars[mine, :] = pack(alpha0, beta, alpha1)
    to_snp(scalars, c_s, c_r)
    q_share = d_share * w_share + ped + scale * genomic_in(1)
    w1_share = w_share - alpha0 * q_share
    result[mine, :] = (r_share - alpha1 * (w1_share + beta * w_share)).astype(BF16)
    to_snp(result, f_s, f_r)
    all_of(w_full, w_s, w_r).wait()
    all_of(scalars, c_s, c_r).wait()
    alpha0, beta, alpha1 = (scalars[:, i : i + 1] for i in range(3))
    b_full = field_t[...]
    x_out[...] = (
        alpha0 * b_full + alpha1 * ((b_full - alpha0 * w_full[...]) + beta * b_full)
    ).T
    all_of(result, f_s, f_r).wait()
    r_out[...] = result[...].astype(F32).T

    for op in range(2):
        for sub in range(SUBS):
            here = spot(sub)
            for k in range(1, Y):
                settle(
                    y_send.at[op, :, y_lanes(0, sub)], y_s.at[op, k - 1, sub], y_r.at[op, 0, sub], at_y(k)
                ).wait_send()
                settle(
                    effects.at[op, :, y_lanes(y, sub)],
                    yg_s.at[op, k - 1, sub], yg_r.at[op, 0, sub], at_y(k),
                ).wait_send()
            settle(
                z_send.at[op, 0 : COLS - ZSHARE, here], z_s.at[op, sub], z_r.at[op, sub], at_z(1)
            ).wait_send()
            settle(
                effects.at[op, 0 : COLS - ZSHARE, y_lanes(y, sub)],
                zg_s.at[op, sub], zg_r.at[op, sub], at_z(1),
            ).wait_send()
        settle(g_send.at[op, 0 : COLS - SHARE, :], g_s.at[op], g_r.at[op], at_s(1)).wait_send()
        for leg in range(2):
            settle(
                p_recv.at[op, leg, 0 : OWN - 1, 0 : depth(op)],
                p_s.at[op, leg], p_r.at[op, leg], at_a(1),
            ).wait_send()
    settle(field.at[1, 0 : COLS - SHARE, :], x_s, x_r, at_s(1)).wait_send()
    settle(norm_recv.at[0 : S - 1], n_s, n_r, at_s(1)).wait_send()


def put_out(x, r, x_out, r_out):
    x_out[...] = x[...]
    r_out[...] = r[...]


def local(geno, freq, rhs, diag, mend, weight, send_rows, sire, dam):
    vmem = pl.BlockSpec(memory_space=pltpu.VMEM)
    dma = pltpu.SemaphoreType.DMA
    results = pl.pallas_call(
        kernel,
        out_shape=(jax.ShapeDtypeStruct((ROWS, COLS), F32),) * 2,
        in_specs=[pl.BlockSpec(memory_space=pl.ANY)] + [vmem] * 8,
        out_specs=(vmem, vmem),
        scratch_shapes=[
            pltpu.VMEM((ROWS, LOCAL), BF16),
            pltpu.VMEM((ROWS, OWN * SLOTS), BF16),
            pltpu.VMEM((OWN * SLOTS, ROWS), BF16),
            pltpu.VMEM((2, COLS, ROWS), BF16),
            pltpu.VMEM((COLS, ROWS), F32),
            pltpu.VMEM((COLS, ROWS), F32),
            pltpu.VMEM((COLS, LOCAL), F32),
            pltpu.VMEM((2, COLS, LOCAL), BF16),
            pltpu.VMEM((2, Y, COLS, YCH), BF16),
            pltpu.VMEM((COLS, YCH), F32),
            pltpu.VMEM((2, COLS, YCH), BF16),
            pltpu.VMEM((2, Z, ZSHARE, YCH), BF16),
            pltpu.VMEM((2, COLS, LOCAL), BF16),
            pltpu.VMEM((COLS, ROWS), F32),
            pltpu.VMEM((2, COLS, ROWS), BF16),
            pltpu.VMEM((2, S, SHARE, ROWS), BF16),
            pltpu.VMEM((2, 2, OWN, 2 * SHARE, 2 * SLOTS), BF16),
            pltpu.VMEM((2, 2, OWN, 2 * SHARE, 2 * SLOTS), BF16),
            pltpu.VMEM((2 * SHARE, OWN * SLOTS), BF16),
            pltpu.VMEM((COLS, ROWS), F32),
            pltpu.VMEM((COLS, ROWS), BF16),
            pltpu.VMEM((COLS, 128), F32),
            pltpu.VMEM((COLS, 128), F32),
            pltpu.VMEM((COLS, 128), F32),
            pltpu.VMEM((S, SHARE, 128), F32),
            dma((SUBS,)),
            dma((2, Y - 1, SUBS)), dma((2, Y, SUBS)),
            dma((2, SUBS)), dma((2, SUBS)),
            dma((2, SUBS)), dma((2, SUBS)),
            dma((2, Y - 1, SUBS)), dma((2, Y, SUBS)),
            dma((2,)), dma((2,)),
            dma, dma,
            dma((2, 2)), dma((2, 2)),
            dma, dma,
            dma, dma,
            dma, dma,
            dma, dma,
        ],
        compiler_params=pltpu.CompilerParams(
            collective_id=0, has_side_effects=True, vmem_limit_bytes=56 * 2**20
        ),
        cost_estimate=pl.CostEstimate(
            flops=5_000_000_000, bytes_accessed=12_000_000, transcendentals=0
        ),
    )(
        geno,
        freq.reshape(1, LOCAL),
        rhs,
        diag,
        mend.reshape(1, ROWS),
        weight.reshape(1, COLS),
        send_rows[0],
        sire.reshape(1, ROWS),
        dam.reshape(1, ROWS),
    )
    half = pl.BlockSpec((ROWS // 2, COLS), lambda i: (i, 0))
    return pl.pallas_call(
        put_out,
        grid=(2,),
        out_shape=(jax.ShapeDtypeStruct((ROWS, COLS), F32),) * 2,
        in_specs=[half] * 2,
        out_specs=(half,) * 2,
    )(*results)


def solution(mesh):
    placed = (
        P("animal", "snp"),
        P("snp"),
        P("animal", None),
        P("animal", None),
        P("animal"),
        P(),
        P("animal", None, None),
        P("animal"),
        P("animal"),
    )
    return jax.shard_map(
        local,
        mesh=mesh,
        in_specs=placed,
        out_specs=(P("animal", None), P("animal", None)),
        check_vma=False,
    )
```

```python
import functools

import jax
import jax.numpy as jnp
from jax import lax
from jax.experimental import pallas as pl
from jax.experimental.pallas import tpu as pltpu
from jax.sharding import PartitionSpec as P

MESH = pl.DeviceIdType.MESH
SNPS = 32768
Z, Y, S = 8, 4, 8
OWN = Z * Y
COLS, ROWS, LOCAL = 128, 1024, 4096
SHARE = COLS // S
ZSHARE = COLS // Z
YCH = LOCAL // Y
SUBS = 4
LAST = SUBS - 1
SUB = YCH // SUBS
SLOTS = 64
PARTS = 3
NT = (((1,), (1,)), ((), ()))
F32, BF16 = jnp.float32, jnp.bfloat16


def dot(a, b):
    return jnp.dot(a, b, preferred_element_type=F32)


def dot_nt(a, b):
    return lax.dot_general(a, b, NT, preferred_element_type=F32)


def halves(value):
    high = value.astype(BF16)
    low = (value - high.astype(F32)).astype(BF16)
    return jnp.concatenate([high, low], axis=0)


def swap(value):
    return pltpu.roll(value, SLOTS, 1)


def kernel(
    geno, freq, rhs, diag, mend, weight, rows, sire, dam,
    x_out, r_out,
    block, send_hot, parent_hot, field, field_t, diag_t,
    y_own, y_send, y_recv, z_own, z_send, z_recv, effects,
    g_own, g_send, g_recv, p_send, p_half, p_recv, p_mat,
    w_full, result, scalars, norm, norm_send, norm_recv, turn_recv, turn_own, turn_send, turn_end,
    load_sem, y_s, y_r, z_s, z_r, zg_s, zg_r, yg_s, yg_r, g_s, g_r, x_s, x_r,
    p_s, p_r, w_s, w_r, c_s, c_r, f_s, f_r, n_s, n_r,
    h_s, h_r, tz_s, tz_r, ty_s, ty_r, tyg_s, tyg_r, tzg_s, tzg_r,
):
    a, s = lax.axis_index("animal"), lax.axis_index("snp")
    z, y = a // Y, a % Y

    def at_y(k):
        return (z * Y + (y + k) % Y, s)

    def at_z(k):
        return (((z + k) % Z) * Y + y, s)

    def at_s(k):
        return (a, (s + k) % S)

    def remote(src, dst, send_sem, recv_sem, peer):
        return pltpu.make_async_remote_copy(
            src_ref=src, dst_ref=dst, send_sem=send_sem, recv_sem=recv_sem,
            device_id=peer, device_id_type=MESH,
        )

    def settle(ref, send_sem, recv_sem, peer):
        return remote(ref, ref, send_sem, recv_sem, peer)

    def y_lanes(which, sub):
        return pl.ds(pl.multiple_of(sub * YCH + which * SUB, SUB), SUB)

    def chunk(sub):
        return slice(sub * YCH, (sub + 1) * YCH)

    def loads(sub):
        return pltpu.make_async_copy(
            geno.at[:, chunk(sub)], block.at[:, chunk(sub)], load_sem.at[sub]
        )

    for sub in range(SUBS):
        loads(sub).start()

    barrier = pltpu.get_barrier_semaphore()

    for peers, count in ((at_y, Y), (at_z, Z), (at_s, S)):
        for k in range(1, count):
            pl.semaphore_signal(barrier, inc=1, device_id=peers(k), device_id_type=MESH)

    field_t[...] = rhs[...].T
    field[0] = field_t[...].astype(BF16)
    mine = pl.ds(pl.multiple_of(s * SHARE, SHARE), SHARE)
    z_mine = pl.ds(pl.multiple_of(z * ZSHARE, ZSHARE), ZSHARE)
    b_share = field_t[mine, :]
    lane = lax.broadcasted_iota(jnp.int32, (SHARE, 2 * SLOTS), 1)
    place = lax.broadcasted_iota(jnp.int32, (SHARE, COLS), 0) + s * SHARE
    scale = jnp.sum(
        jnp.where(lane == place, weight[...], 0.0), axis=1, keepdims=True
    ) * (1.0 / SNPS)
    first = lane < SLOTS

    def centre(sub):
        loads(sub).wait()
        lanes = chunk(sub)
        twice = 2.0 * freq[:, lanes]

        def rows_of(i, carry):
            at = pl.ds(pl.multiple_of(i * 128, 128), 128)
            block[at, lanes] = (block[at, lanes].astype(F32) - twice).astype(BF16)
            return carry

        lax.fori_loop(0, ROWS // 128, rows_of, 0)

    def spot(sub):
        return slice(sub * SUB, (sub + 1) * SUB)

    def effects_send(op, sub):
        for k in range(1, Y):
            remote(
                y_send.at[op, :, y_lanes((y + k) % Y, sub)], y_recv.at[op, y, :, spot(sub)],
                y_s.at[op, k - 1, sub], y_r.at[op, y, sub], at_y(k),
            ).start()

    def effects_out(op, sub, send=True):
        if op == 0:
            centre(sub)
        value = dot(field[op], block[:, chunk(sub)])
        y_send[op, :, chunk(sub)] = value.astype(BF16)
        if send:
            effects_send(op, sub)
        y_own[:, chunk(sub)] = value

    def effects_mid(op, sub):
        here = spot(sub)
        total = y_own[:, y_lanes(y, sub)]
        for k in range(1, Y):
            which = (y + k) % Y
            piece = y_recv.at[op, which, :, here]
            settle(piece, y_s.at[op, k - 1, sub], y_r.at[op, which, sub], at_y(k)).wait_recv()
            total = total + piece[...].astype(F32)
        z_own[:, here] = total
        z_send[op, :, here] = total.astype(BF16)

        def give(k, carry):
            peer_rows = pl.ds(pl.multiple_of(((z + k) % Z) * ZSHARE, ZSHARE), ZSHARE)
            remote(
                z_send.at[op, peer_rows, here], z_recv.at[op, z, :, here],
                z_s.at[op, sub], z_r.at[op, sub], at_z(k),
            ).start()
            return carry

        lax.fori_loop(1, Z, give, 0)

    def effects_sum(op, sub):
        here = spot(sub)
        settle(
            z_recv.at[op, 0 : Z - 1, :, here], z_s.at[op, sub], z_r.at[op, sub], at_z(1)
        ).wait_recv()
        total = z_own[z_mine, here]
        for k in range(1, Z):
            total = total + z_recv[op, (z + k) % Z, :, here].astype(F32)
        effects[op, z_mine, y_lanes(y, sub)] = total.astype(BF16)

        def give(k, carry):
            piece = effects.at[op, z_mine, y_lanes(y, sub)]
            remote(piece, piece, zg_s.at[op, sub], zg_r.at[op, sub], at_z(k)).start()
            return carry

        lax.fori_loop(1, Z, give, 0)

    def turn_out(op):
        def give(k, carry):
            peer_rows = pl.ds(pl.multiple_of(((z + k) % Z) * ZSHARE, ZSHARE), ZSHARE)
            remote(
                y_send.at[op, peer_rows, chunk(LAST)], turn_recv.at[op, z],
                tz_s.at[op], tz_r.at[op], at_z(k),
            ).start()
            return carry

        lax.fori_loop(1, Z, give, 0)

    def turn_mid(op):
        settle(turn_recv.at[op, 0 : Z - 1], tz_s.at[op], tz_r.at[op], at_z(1)).wait_recv()
        total = y_own[z_mine, chunk(LAST)]
        for k in range(1, Z):
            total = total + turn_recv[op, (z + k) % Z].astype(F32)
        turn_own[...] = total
        turn_send[op] = total.astype(BF16)
        for k in range(1, Y):
            lanes = pl.ds(pl.multiple_of(((y + k) % Y) * SUB, SUB), SUB)
            remote(
                turn_send.at[op, :, lanes], turn_end.at[op, y], ty_s.at[op], ty_r.at[op], at_y(k)
            ).start()

    def turn_sum(op):
        settle(turn_end.at[op, 0 : Y - 1], ty_s.at[op], ty_r.at[op], at_y(1)).wait_recv()
        total = turn_own[:, pl.ds(pl.multiple_of(y * SUB, SUB), SUB)]
        for k in range(1, Y):
            total = total + turn_end[op, (y + k) % Y].astype(F32)
        effects[op, z_mine, y_lanes(y, LAST)] = total.astype(BF16)
        for k in range(1, Y):
            piece = effects.at[op, z_mine, y_lanes(y, LAST)]
            remote(piece, piece, tyg_s.at[op], tyg_r.at[op], at_y(k)).start()

    def turn_rows(op):
        return settle(
            effects.at[op, 0 : (Y - 1) * ZSHARE, y_lanes(y, LAST)],
            tyg_s.at[op], tyg_r.at[op], at_y(1),
        )

    def turn_all(op):
        return settle(
            effects.at[op, 0 : COLS - ZSHARE, chunk(LAST)], tzg_s.at[op], tzg_r.at[op], at_z(1)
        )

    def turn_spread(op):
        turn_rows(op).wait_recv()

        def give(k, carry):
            piece = effects.at[op, z_mine, chunk(LAST)]
            remote(piece, piece, tzg_s.at[op], tzg_r.at[op], at_z(k)).start()
            return carry

        lax.fori_loop(1, Z, give, 0)

    def effects_spread(op, sub):
        lanes = y_lanes(y, sub)
        settle(
            effects.at[op, 0 : COLS - ZSHARE, lanes], zg_s.at[op, sub], zg_r.at[op, sub], at_z(1)
        ).wait_recv()
        for k in range(1, Y):
            piece = effects.at[op, :, lanes]
            remote(piece, piece, yg_s.at[op, k - 1, sub], yg_r.at[op, y, sub], at_y(k)).start()

    def take(op, sub):
        if sub == LAST:
            turn_all(op).wait_recv()
        for k in range(1, Y if sub < LAST else 1):
            which = (y + k) % Y
            settle(
                effects.at[op, :, y_lanes(which, sub)],
                yg_s.at[op, k - 1, sub], yg_r.at[op, which, sub], at_y(k),
            ).wait_recv()
        piece = effects[op, :, chunk(sub)]
        value = dot_nt(piece, block[:, chunk(sub)])
        if sub == 0:
            g_own[...] = value
        else:
            g_own[...] += value
        if op == 1:
            square = jnp.zeros((COLS, 128), F32)
            for part in range(YCH // 128):
                one = piece[:, part * 128 : (part + 1) * 128].astype(F32)
                square = square + one * one
            if sub == 0:
                norm[...] = square
            else:
                norm[...] += square

    def genomic_out(op):
        g_send[op] = g_own[...].astype(BF16)
        if op == 1:
            norm_send[...] = jnp.broadcast_to(
                jnp.sum(norm[...], axis=1, keepdims=True), (COLS, 128)
            )

        def give(k, carry):
            peer_rows = pl.ds(pl.multiple_of(((s + k) % S) * SHARE, SHARE), SHARE)
            if op == 1:
                remote(norm_send.at[peer_rows, :], norm_recv.at[s], n_s, n_r, at_s(k)).start()
            remote(
                g_send.at[op, peer_rows, :], g_recv.at[op, s], g_s.at[op], g_r.at[op], at_s(k)
            ).start()
            return carry

        lax.fori_loop(1, S, give, 0)

    def genomic_in(op):
        settle(g_recv.at[op, 0 : S - 1], g_s.at[op], g_r.at[op], at_s(1)).wait_recv()
        total = g_own[mine, :]
        for k in range(1, S):
            total = total + g_recv[op, (s + k) % S].astype(F32)
        return total

    def norm_in():
        settle(norm_recv.at[0 : S - 1], n_s, n_r, at_s(1)).wait_recv()
        total = norm_send[mine, :]
        for k in range(1, S):
            total = total + norm_recv[(s + k) % S]
        return total[:, 0:1]

    def pack(*columns):
        tile = jnp.zeros((SHARE, 128), F32)
        for position, column in enumerate(columns):
            tile = jnp.where(lane == position, column, tile)
        return tile

    def depth(op):
        return 2 * SHARE if op == 1 else SHARE

    def relay_out(leg, op, both, products=()):
        for pair in range(OWN // 2):
            lanes = slice(pair * 2 * SLOTS, (pair + 1) * 2 * SLOTS)
            high, low = both[:SHARE, lanes], both[SHARE:, lanes]
            p_send[op, leg, 2 * pair // Y, 2 * pair % Y, :SHARE] = jnp.where(first, high, swap(low)).astype(BF16)
            p_send[op, leg, 2 * pair // Y, 2 * pair % Y + 1, :SHARE] = jnp.where(first, swap(high), low).astype(BF16)
        if products:
            parts = []
            for product in products:
                left = jnp.sum(product, axis=1, keepdims=True)
                for _ in range(PARTS):
                    part = left.astype(BF16).astype(F32)
                    left = left - part
                    parts.append(part)
            tile = pack(*parts).astype(BF16)
            for peer in range(OWN):
                p_send[op, leg, peer // Y, peer % Y, SHARE:] = tile

    def relay_y(leg, op):
        return settle(
            p_half.at[op, leg, 0 : Y - 1, :, 0 : depth(op)],
            p_s.at[op, leg], p_r.at[op, leg], at_y(1),
        )

    def relay_z(leg, op):
        return settle(
            p_recv.at[op, leg, 0 : OWN - Y, 0 : depth(op)], h_s.at[op, leg], h_r.at[op, leg], at_z(1)
        )

    def relay_send(leg, op):
        for k in range(1, Y):
            remote(
                p_send.at[op, leg, :, (y + k) % Y, 0 : depth(op)],
                p_half.at[op, leg, y, :, 0 : depth(op)],
                p_s.at[op, leg], p_r.at[op, leg], at_y(k),
            ).start()
        p_half[op, leg, y, :, : depth(op)] = p_send[op, leg, :, y, : depth(op)]

    def relay_turn(leg, op):
        relay_y(leg, op).wait_recv()
        own = pl.ds(z * Y, Y)

        def give(k, carry):
            remote(
                p_half.at[op, leg, :, (z + k) % Z, 0 : depth(op)],
                p_recv.at[op, leg, own, 0 : depth(op)],
                h_s.at[op, leg], h_r.at[op, leg], at_z(k),
            ).start()
            return carry

        lax.fori_loop(1, Z, give, 0)
        p_recv[op, leg, own, : depth(op)] = p_half[op, leg, :, z, : depth(op)]

    def relay_in(leg, op):
        relay_z(leg, op).wait_recv()
        for pair in range(OWN // 2):
            lanes = slice(pair * 2 * SLOTS, (pair + 1) * 2 * SLOTS)
            one = p_recv[op, leg, 2 * pair, :SHARE].astype(F32)
            two = p_recv[op, leg, 2 * pair + 1, :SHARE].astype(F32)
            p_mat[:SHARE, lanes] = jnp.where(first, one, swap(two)).astype(BF16)
            p_mat[SHARE:, lanes] = jnp.where(first, swap(one), two).astype(BF16)
        return p_mat[...]

    def totals(leg):
        tile = jnp.sum(p_recv[1, leg, :, SHARE:, :].astype(F32), axis=0)
        return tuple(
            jnp.sum(tile[:, i * PARTS : (i + 1) * PARTS], axis=1, keepdims=True) for i in range(3)
        )

    def fold(both):
        return both[:SHARE] + both[SHARE:]

    def make_send_hot():
        even = rows[pl.ds(0, OWN // 2, stride=2), :]
        odd = rows[pl.ds(1, OWN // 2, stride=2), :]
        pairs = jnp.concatenate([even, odd], axis=1)
        at = lax.broadcasted_iota(jnp.int32, (ROWS, 2 * SLOTS), 0)
        for pair in range(OWN // 2):
            lanes = slice(pair * 2 * SLOTS, (pair + 1) * 2 * SLOTS)
            send_hot[:, lanes] = (at == pairs[pair : pair + 1, :]).astype(F32).astype(BF16)

    def make_parent_hot():
        def some(i, carry):
            at = lax.broadcasted_iota(jnp.int32, (128, ROWS), 0) + i * 128
            here = (at == sire[...]) | (at == dam[...])
            parent_hot[pl.ds(pl.multiple_of(i * 128, 128), 128), :] = here.astype(F32).astype(BF16)
            return carry

        lax.fori_loop(0, OWN * SLOTS // 128, some, 0)

    def pedigree_out(op, value, products=()):
        relay_out(0, op, dot(halves(value), send_hot[...]), products)

    def pedigree_mid(op, value):
        parents = fold(dot(relay_in(0, op), parent_hot[...]))
        lacks = value - 0.5 * parents
        return lacks, mend[...] * lacks

    def pedigree_back(op, value, lacks, term):
        back = -0.5 * fold(dot_nt(halves(term), parent_hot[...]))
        high = back.astype(BF16).astype(F32)
        both = jnp.concatenate([high, back - high], axis=0)
        if op == 0:
            relay_out(1, op, both)
            relay_send(1, op)
            return ()
        gamma, delta, square = totals(0)
        alpha = gamma / delta
        rest = b_share - alpha * value
        relay_out(
            1, op, both, (rest * rest, rest * value, d_share * value * value + term * lacks)
        )
        relay_send(1, op)
        return gamma, alpha, square, rest

    def pedigree_end(op, term):
        return term + fold(dot_nt(relay_in(1, op), send_hot[...]))

    def share_field(value):
        field[1, mine, :] = value.astype(BF16)

        def give(k, carry):
            piece = field.at[1, mine, :]
            remote(piece, piece, x_s, x_r, at_s(k)).start()
            return carry

        lax.fori_loop(1, S, give, 0)

    def field_arrives():
        settle(field.at[1, 0 : COLS - SHARE, :], x_s, x_r, at_s(1)).wait_recv()

    def to_snp(ref, send_sem, recv_sem):
        def give(k, carry):
            piece = ref.at[mine, :]
            remote(piece, piece, send_sem, recv_sem, at_s(k)).start()
            return carry

        lax.fori_loop(1, S, give, 0)

    def all_of(ref, send_sem, recv_sem):
        return settle(ref.at[0 : COLS - SHARE, :], send_sem, recv_sem, at_s(1))

    for sub in range(SUBS):
        effects_out(0, sub, send=False)
    make_send_hot()
    pedigree_out(0, b_share)
    pl.semaphore_wait(barrier, Y - 1 + Z - 1 + S - 1)
    turn_out(0)
    effects_send(0, 0)
    relay_send(0, 0)
    effects_send(0, 1)
    make_parent_hot()
    diag_t[...] = diag[...].T
    d_share = diag_t[mine, :]
    effects_mid(0, 0)
    effects_send(0, 2)
    relay_turn(0, 0)
    effects_mid(0, 1)
    turn_mid(0)
    effects_mid(0, 2)
    effects_sum(0, 0)
    effects_sum(0, 1)
    turn_sum(0)
    lacks, term = pedigree_mid(0, b_share)
    effects_spread(0, 0)
    effects_sum(0, 2)
    turn_spread(0)
    pedigree_back(0, b_share, lacks, term)
    effects_spread(0, 1)
    effects_spread(0, 2)
    relay_turn(1, 0)
    take(0, 0)
    take(0, 1)
    take(0, 2)
    take(0, 3)
    genomic_out(0)
    ped = pedigree_end(0, term)
    w_share = d_share * b_share + ped
    w_share = w_share + scale * genomic_in(0)
    share_field(w_share)
    pedigree_out(1, w_share, (b_share * b_share, w_share * b_share, w_share * w_share))
    relay_send(0, 1)
    w_full[mine, :] = w_share
    field_arrives()

    effects_out(1, 3, send=False)
    turn_out(1)
    effects_out(1, 0)
    effects_out(1, 1)
    effects_out(1, 2, send=False)
    relay_turn(0, 1)
    effects_mid(1, 0)
    effects_send(1, 2)
    to_snp(w_full, w_s, w_r)
    effects_mid(1, 1)
    lacks, term = pedigree_mid(1, w_share)
    turn_mid(1)
    effects_mid(1, 2)
    effects_sum(1, 0)
    effects_sum(1, 1)
    turn_sum(1)
    gamma0, alpha0, square0, r_share = pedigree_back(1, w_share, lacks, term)
    effects_spread(1, 0)
    effects_sum(1, 2)
    turn_spread(1)
    effects_spread(1, 1)
    relay_turn(1, 1)
    effects_spread(1, 2)
    take(1, 0)
    take(1, 1)
    take(1, 2)
    take(1, 3)
    genomic_out(1)
    ped = pedigree_end(1, term)
    gamma1, cross, quad = totals(1)
    beta = gamma1 / gamma0
    quad = quad + scale * norm_in()
    delta1 = cross - alpha0 * (square0 - alpha0 * quad)
    alpha1 = gamma1 / (delta1 - beta * gamma1 / alpha0)
    scalars[mine, :] = pack(alpha0, beta, alpha1)
    to_snp(scalars, c_s, c_r)
    q_share = d_share * w_share + ped + scale * genomic_in(1)
    w1_share = w_share - alpha0 * q_share
    result[mine, :] = (r_share - alpha1 * (w1_share + beta * w_share)).astype(BF16)
    to_snp(result, f_s, f_r)
    all_of(w_full, w_s, w_r).wait()
    all_of(scalars, c_s, c_r).wait()
    alpha0, beta, alpha1 = (scalars[:, i : i + 1] for i in range(3))
    b_full = field_t[...]
    x_out[...] = (
        alpha0 * b_full + alpha1 * ((b_full - alpha0 * w_full[...]) + beta * b_full)
    ).T
    all_of(result, f_s, f_r).wait()
    r_out[...] = result[...].astype(F32).T

    for op in range(2):
        settle(turn_recv.at[op, 0 : Z - 1], tz_s.at[op], tz_r.at[op], at_z(1)).wait_send()
        settle(turn_end.at[op, 0 : Y - 1], ty_s.at[op], ty_r.at[op], at_y(1)).wait_send()
        turn_rows(op).wait_send()
        turn_all(op).wait_send()
        for sub in range(LAST):
            here = spot(sub)
            for k in range(1, Y):
                settle(
                    y_send.at[op, :, y_lanes(0, sub)], y_s.at[op, k - 1, sub], y_r.at[op, 0, sub], at_y(k)
                ).wait_send()
                settle(
                    effects.at[op, :, y_lanes(y, sub)],
                    yg_s.at[op, k - 1, sub], yg_r.at[op, 0, sub], at_y(k),
                ).wait_send()
            settle(
                z_send.at[op, 0 : COLS - ZSHARE, here], z_s.at[op, sub], z_r.at[op, sub], at_z(1)
            ).wait_send()
            settle(
                effects.at[op, 0 : COLS - ZSHARE, y_lanes(y, sub)],
                zg_s.at[op, sub], zg_r.at[op, sub], at_z(1),
            ).wait_send()
        settle(g_send.at[op, 0 : COLS - SHARE, :], g_s.at[op], g_r.at[op], at_s(1)).wait_send()
        for leg in range(2):
            relay_y(leg, op).wait_send()
            relay_z(leg, op).wait_send()
    settle(field.at[1, 0 : COLS - SHARE, :], x_s, x_r, at_s(1)).wait_send()
    settle(norm_recv.at[0 : S - 1], n_s, n_r, at_s(1)).wait_send()


def put_out(x, r, x_out, r_out):
    x_out[...] = x[...]
    r_out[...] = r[...]


def local(geno, freq, rhs, diag, mend, weight, send_rows, sire, dam):
    vmem = pl.BlockSpec(memory_space=pltpu.VMEM)
    dma = pltpu.SemaphoreType.DMA
    results = pl.pallas_call(
        kernel,
        out_shape=(jax.ShapeDtypeStruct((ROWS, COLS), F32),) * 2,
        in_specs=[pl.BlockSpec(memory_space=pl.ANY)] + [vmem] * 8,
        out_specs=(vmem, vmem),
        scratch_shapes=[
            pltpu.VMEM((ROWS, LOCAL), BF16),
            pltpu.VMEM((ROWS, OWN * SLOTS), BF16),
            pltpu.VMEM((OWN * SLOTS, ROWS), BF16),
            pltpu.VMEM((2, COLS, ROWS), BF16),
            pltpu.VMEM((COLS, ROWS), F32),
            pltpu.VMEM((COLS, ROWS), F32),
            pltpu.VMEM((COLS, LOCAL), F32),
            pltpu.VMEM((2, COLS, LOCAL), BF16),
            pltpu.VMEM((2, Y, COLS, YCH), BF16),
            pltpu.VMEM((COLS, YCH), F32),
            pltpu.VMEM((2, COLS, YCH), BF16),
            pltpu.VMEM((2, Z, ZSHARE, YCH), BF16),
            pltpu.VMEM((2, COLS, LOCAL), BF16),
            pltpu.VMEM((COLS, ROWS), F32),
            pltpu.VMEM((2, COLS, ROWS), BF16),
            pltpu.VMEM((2, S, SHARE, ROWS), BF16),
            pltpu.VMEM((2, 2, Z, Y, 2 * SHARE, 2 * SLOTS), BF16),
            pltpu.VMEM((2, 2, Y, Z, 2 * SHARE, 2 * SLOTS), BF16),
            pltpu.VMEM((2, 2, OWN, 2 * SHARE, 2 * SLOTS), BF16),
            pltpu.VMEM((2 * SHARE, OWN * SLOTS), BF16),
            pltpu.VMEM((COLS, ROWS), F32),
            pltpu.VMEM((COLS, ROWS), BF16),
            pltpu.VMEM((COLS, 128), F32),
            pltpu.VMEM((COLS, 128), F32),
            pltpu.VMEM((COLS, 128), F32),
            pltpu.VMEM((S, SHARE, 128), F32),
            pltpu.VMEM((2, Z, ZSHARE, YCH), BF16),
            pltpu.VMEM((ZSHARE, YCH), F32),
            pltpu.VMEM((2, ZSHARE, YCH), BF16),
            pltpu.VMEM((2, Y, ZSHARE, SUB), BF16),
            dma((SUBS,)),
            dma((2, Y - 1, SUBS)), dma((2, Y, SUBS)),
            dma((2, SUBS)), dma((2, SUBS)),
            dma((2, SUBS)), dma((2, SUBS)),
            dma((2, Y - 1, SUBS)), dma((2, Y, SUBS)),
            dma((2,)), dma((2,)),
            dma, dma,
            dma((2, 2)), dma((2, 2)),
            dma, dma,
            dma, dma,
            dma, dma,
            dma, dma,
            dma((2, 2)), dma((2, 2)),
            *[dma((2,))] * 8,
        ],
        compiler_params=pltpu.CompilerParams(
            collective_id=0, has_side_effects=True, vmem_limit_bytes=56 * 2**20
        ),
        cost_estimate=pl.CostEstimate(
            flops=5_000_000_000, bytes_accessed=12_000_000, transcendentals=0
        ),
    )(
        geno,
        freq.reshape(1, LOCAL),
        rhs,
        diag,
        mend.reshape(1, ROWS),
        weight.reshape(1, COLS),
        send_rows[0],
        sire.reshape(1, ROWS),
        dam.reshape(1, ROWS),
    )
    half = pl.BlockSpec((ROWS // 2, COLS), lambda i: (i, 0))
    return pl.pallas_call(
        put_out,
        grid=(2,),
        out_shape=(jax.ShapeDtypeStruct((ROWS, COLS), F32),) * 2,
        in_specs=[half] * 2,
        out_specs=(half,) * 2,
    )(*results)


def solution(mesh):
    placed = (
        P("animal", "snp"),
        P("snp"),
        P("animal", None),
        P("animal", None),
        P("animal"),
        P(),
        P("animal", None, None),
        P("animal"),
        P("animal"),
    )
    return jax.shard_map(
        local,
        mesh=mesh,
        in_specs=placed,
        out_specs=(P("animal", None), P("animal", None)),
        check_vma=False,
    )
```

```python
import functools

import jax
import jax.numpy as jnp
from jax import lax
from jax.experimental import pallas as pl
from jax.experimental.pallas import tpu as pltpu
from jax.sharding import PartitionSpec as P

MESH = pl.DeviceIdType.MESH
SNPS = 32768
Z, Y, S = 8, 4, 8
OWN = Z * Y
COLS, ROWS, LOCAL = 128, 1024, 4096
SHARE = COLS // S
ZSHARE = COLS // Z
YCH = LOCAL // Y
SUBS = 4
LAST = SUBS - 1
SUB = YCH // SUBS
SLOTS = 64
PARTS = 3
NT = (((1,), (1,)), ((), ()))
F32, BF16 = jnp.float32, jnp.bfloat16


def dot(a, b):
    return jnp.dot(a, b, preferred_element_type=F32)


def dot_nt(a, b):
    return lax.dot_general(a, b, NT, preferred_element_type=F32)


def halves(value):
    high = value.astype(BF16)
    low = (value - high.astype(F32)).astype(BF16)
    return jnp.concatenate([high, low], axis=0)


def swap(value):
    return pltpu.roll(value, SLOTS, 1)


def kernel(
    geno, freq, rhs, diag, mend, weight, rows, sire, dam,
    x_out, r_out,
    block, send_hot, parent_hot, field, field_t, diag_t,
    y_own, y_send, y_recv, z_own, z_send, z_recv, effects,
    g_own, g_send, g_recv, y_box, z_box, p_mat,
    w_full, result, scalars, norm, norm_send, norm_recv, turn_recv, turn_own, turn_send, turn_end,
    load_sem, y_s, y_r, z_s, z_r, zg_s, zg_r, yg_s, yg_r, g_s, g_r, x_s, x_r,
    p_s, p_r, w_s, w_r, c_s, c_r, f_s, f_r, n_s, n_r,
    h_s, h_r, tz_s, tz_r, ty_s, ty_r, tyg_s, tyg_r, tzg_s, tzg_r,
):
    a, s = lax.axis_index("animal"), lax.axis_index("snp")
    z, y = a // Y, a % Y

    def at_y(k):
        return (z * Y + (y + k) % Y, s)

    def at_z(k):
        return (((z + k) % Z) * Y + y, s)

    def at_s(k):
        return (a, (s + k) % S)

    def remote(src, dst, send_sem, recv_sem, peer):
        return pltpu.make_async_remote_copy(
            src_ref=src, dst_ref=dst, send_sem=send_sem, recv_sem=recv_sem,
            device_id=peer, device_id_type=MESH,
        )

    def settle(ref, send_sem, recv_sem, peer):
        return remote(ref, ref, send_sem, recv_sem, peer)

    def y_lanes(which, sub):
        return pl.ds(pl.multiple_of(sub * YCH + which * SUB, SUB), SUB)

    def chunk(sub):
        return slice(sub * YCH, (sub + 1) * YCH)

    def loads(sub):
        return pltpu.make_async_copy(
            geno.at[:, chunk(sub)], block.at[:, chunk(sub)], load_sem.at[sub]
        )

    for sub in range(SUBS):
        loads(sub).start()

    barrier = pltpu.get_barrier_semaphore()

    for peers, count in ((at_y, Y), (at_z, Z), (at_s, S)):
        for k in range(1, count):
            pl.semaphore_signal(barrier, inc=1, device_id=peers(k), device_id_type=MESH)

    field_t[...] = rhs[...].T
    field[0] = field_t[...].astype(BF16)
    mine = pl.ds(pl.multiple_of(s * SHARE, SHARE), SHARE)
    z_mine = pl.ds(pl.multiple_of(z * ZSHARE, ZSHARE), ZSHARE)
    b_share = field_t[mine, :]
    lane = lax.broadcasted_iota(jnp.int32, (SHARE, 2 * SLOTS), 1)
    place = lax.broadcasted_iota(jnp.int32, (SHARE, COLS), 0) + s * SHARE
    scale = jnp.sum(
        jnp.where(lane == place, weight[...], 0.0), axis=1, keepdims=True
    ) * (1.0 / SNPS)
    first = lane < SLOTS

    def centre(sub):
        loads(sub).wait()
        lanes = chunk(sub)
        twice = 2.0 * freq[:, lanes]

        def rows_of(i, carry):
            at = pl.ds(pl.multiple_of(i * 128, 128), 128)
            block[at, lanes] = (block[at, lanes].astype(F32) - twice).astype(BF16)
            return carry

        lax.fori_loop(0, ROWS // 128, rows_of, 0)

    def spot(sub):
        return slice(sub * SUB, (sub + 1) * SUB)

    def effects_send(op, sub):
        for k in range(1, Y):
            remote(
                y_send.at[op, :, y_lanes((y + k) % Y, sub)], y_recv.at[op, y, :, spot(sub)],
                y_s.at[op, k - 1, sub], y_r.at[op, y, sub], at_y(k),
            ).start()

    def effects_out(op, sub, send=True):
        if op == 0:
            centre(sub)
        value = dot(field[op], block[:, chunk(sub)])
        y_send[op, :, chunk(sub)] = value.astype(BF16)
        if send:
            effects_send(op, sub)
        y_own[:, chunk(sub)] = value

    def effects_mid(op, sub):
        here = spot(sub)
        total = y_own[:, y_lanes(y, sub)]
        for k in range(1, Y):
            which = (y + k) % Y
            piece = y_recv.at[op, which, :, here]
            settle(piece, y_s.at[op, k - 1, sub], y_r.at[op, which, sub], at_y(k)).wait_recv()
            total = total + piece[...].astype(F32)
        z_own[:, here] = total
        z_send[op, :, here] = total.astype(BF16)

        def give(k, carry):
            peer_rows = pl.ds(pl.multiple_of(((z + k) % Z) * ZSHARE, ZSHARE), ZSHARE)
            remote(
                z_send.at[op, peer_rows, here], z_recv.at[op, z, :, here],
                z_s.at[op, sub], z_r.at[op, sub], at_z(k),
            ).start()
            return carry

        lax.fori_loop(1, Z, give, 0)

    def effects_sum(op, sub):
        here = spot(sub)
        settle(
            z_recv.at[op, 0 : Z - 1, :, here], z_s.at[op, sub], z_r.at[op, sub], at_z(1)
        ).wait_recv()
        total = z_own[z_mine, here]
        for k in range(1, Z):
            total = total + z_recv[op, (z + k) % Z, :, here].astype(F32)
        effects[op, z_mine, y_lanes(y, sub)] = total.astype(BF16)

        def give(k, carry):
            piece = effects.at[op, z_mine, y_lanes(y, sub)]
            remote(piece, piece, zg_s.at[op, sub], zg_r.at[op, sub], at_z(k)).start()
            return carry

        lax.fori_loop(1, Z, give, 0)

    def turn_out(op):
        def give(k, carry):
            peer_rows = pl.ds(pl.multiple_of(((z + k) % Z) * ZSHARE, ZSHARE), ZSHARE)
            remote(
                y_send.at[op, peer_rows, chunk(LAST)], turn_recv.at[op, z],
                tz_s.at[op], tz_r.at[op], at_z(k),
            ).start()
            return carry

        lax.fori_loop(1, Z, give, 0)

    def turn_mid(op):
        settle(turn_recv.at[op, 0 : Z - 1], tz_s.at[op], tz_r.at[op], at_z(1)).wait_recv()
        total = y_own[z_mine, chunk(LAST)]
        for k in range(1, Z):
            total = total + turn_recv[op, (z + k) % Z].astype(F32)
        turn_own[...] = total
        turn_send[op] = total.astype(BF16)
        for k in range(1, Y):
            lanes = pl.ds(pl.multiple_of(((y + k) % Y) * SUB, SUB), SUB)
            remote(
                turn_send.at[op, :, lanes], turn_end.at[op, y], ty_s.at[op], ty_r.at[op], at_y(k)
            ).start()

    def turn_sum(op):
        settle(turn_end.at[op, 0 : Y - 1], ty_s.at[op], ty_r.at[op], at_y(1)).wait_recv()
        total = turn_own[:, pl.ds(pl.multiple_of(y * SUB, SUB), SUB)]
        for k in range(1, Y):
            total = total + turn_end[op, (y + k) % Y].astype(F32)
        effects[op, z_mine, y_lanes(y, LAST)] = total.astype(BF16)
        for k in range(1, Y):
            piece = effects.at[op, z_mine, y_lanes(y, LAST)]
            remote(piece, piece, tyg_s.at[op], tyg_r.at[op], at_y(k)).start()

    def turn_rows(op):
        return settle(
            effects.at[op, 0 : (Y - 1) * ZSHARE, y_lanes(y, LAST)],
            tyg_s.at[op], tyg_r.at[op], at_y(1),
        )

    def turn_all(op):
        return settle(
            effects.at[op, 0 : COLS - ZSHARE, chunk(LAST)], tzg_s.at[op], tzg_r.at[op], at_z(1)
        )

    def turn_spread(op):
        turn_rows(op).wait_recv()

        def give(k, carry):
            piece = effects.at[op, z_mine, chunk(LAST)]
            remote(piece, piece, tzg_s.at[op], tzg_r.at[op], at_z(k)).start()
            return carry

        lax.fori_loop(1, Z, give, 0)

    def effects_spread(op, sub):
        lanes = y_lanes(y, sub)
        settle(
            effects.at[op, 0 : COLS - ZSHARE, lanes], zg_s.at[op, sub], zg_r.at[op, sub], at_z(1)
        ).wait_recv()
        for k in range(1, Y):
            piece = effects.at[op, :, lanes]
            remote(piece, piece, yg_s.at[op, k - 1, sub], yg_r.at[op, y, sub], at_y(k)).start()

    def take(op, sub):
        if sub == LAST:
            turn_all(op).wait_recv()
        for k in range(1, Y if sub < LAST else 1):
            which = (y + k) % Y
            settle(
                effects.at[op, :, y_lanes(which, sub)],
                yg_s.at[op, k - 1, sub], yg_r.at[op, which, sub], at_y(k),
            ).wait_recv()
        piece = effects[op, :, chunk(sub)]
        value = dot_nt(piece, block[:, chunk(sub)])
        if sub == 0:
            g_own[...] = value
        else:
            g_own[...] += value
        if op == 1:
            square = jnp.zeros((COLS, 128), F32)
            for part in range(YCH // 128):
                one = piece[:, part * 128 : (part + 1) * 128].astype(F32)
                square = square + one * one
            if sub == 0:
                norm[...] = square
            else:
                norm[...] += square

    def genomic_out(op):
        g_send[op] = g_own[...].astype(BF16)
        if op == 1:
            norm_send[...] = jnp.broadcast_to(
                jnp.sum(norm[...], axis=1, keepdims=True), (COLS, 128)
            )

        def give(k, carry):
            peer_rows = pl.ds(pl.multiple_of(((s + k) % S) * SHARE, SHARE), SHARE)
            if op == 1:
                remote(norm_send.at[peer_rows, :], norm_recv.at[s], n_s, n_r, at_s(k)).start()
            remote(
                g_send.at[op, peer_rows, :], g_recv.at[op, s], g_s.at[op], g_r.at[op], at_s(k)
            ).start()
            return carry

        lax.fori_loop(1, S, give, 0)

    def genomic_in(op):
        settle(g_recv.at[op, 0 : S - 1], g_s.at[op], g_r.at[op], at_s(1)).wait_recv()
        total = g_own[mine, :]
        for k in range(1, S):
            total = total + g_recv[op, (s + k) % S].astype(F32)
        return total

    def norm_in():
        settle(norm_recv.at[0 : S - 1], n_s, n_r, at_s(1)).wait_recv()
        total = norm_send[mine, :]
        for k in range(1, S):
            total = total + norm_recv[(s + k) % S]
        return total[:, 0:1]

    def pack(*columns):
        tile = jnp.zeros((SHARE, 128), F32)
        for position, column in enumerate(columns):
            tile = jnp.where(lane == position, column, tile)
        return tile

    def in_y(op):
        return Z + 1 if op == 1 else Z

    def in_z(op):
        return Y + 1 if op == 1 else Y

    def split(columns):
        parts = []
        for left in columns:
            for _ in range(PARTS):
                part = left.astype(BF16).astype(F32)
                left = left - part
                parts.append(part)
        return pack(*parts).astype(BF16)

    def column_sums(products):
        return [jnp.sum(p, axis=1, keepdims=True) for p in products]

    def joined(tiles):
        tile = jnp.sum(tiles.astype(F32), axis=0)
        return tuple(
            jnp.sum(tile[:, i * PARTS : (i + 1) * PARTS], axis=1, keepdims=True) for i in range(3)
        )

    def y_waits(leg, op):
        return settle(
            y_box.at[op, 2 * leg + 1, 0 : Y - 1, 0 : in_y(op)],
            p_s.at[op, leg], p_r.at[op, leg], at_y(1),
        )

    def z_waits(leg, op):
        return settle(
            z_box.at[op, 2 * leg + 1, 0 : Z - 1, 0 : in_z(op)],
            h_s.at[op, leg], h_r.at[op, leg], at_z(1),
        )

    def along_y(leg, op):
        size = in_y(op)
        for k in range(1, Y):
            remote(
                y_box.at[op, 2 * leg, (y + k) % Y, 0:size],
                y_box.at[op, 2 * leg + 1, y, 0:size],
                p_s.at[op, leg], p_r.at[op, leg], at_y(k),
            ).start()
        y_box[op, 2 * leg + 1, y, :size] = y_box[op, 2 * leg, y, :size]

    def along_z(leg, op):
        size = in_z(op)

        def give(k, carry):
            remote(
                z_box.at[op, 2 * leg, (z + k) % Z, 0:size],
                z_box.at[op, 2 * leg + 1, z, 0:size],
                h_s.at[op, leg], h_r.at[op, leg], at_z(k),
            ).start()
            return carry

        lax.fori_loop(1, Z, give, 0)
        z_box[op, 2 * leg + 1, z, :size] = z_box[op, 2 * leg, z, :size]

    def regroup(one, two):
        one, two = one.astype(F32), two.astype(F32)
        return (
            jnp.where(first, one, swap(two)).astype(BF16),
            jnp.where(first, swap(one), two).astype(BF16),
        )

    def relay_out(op, tiles, products=()):
        for i in range(OWN // 2):
            lanes = slice(i * 128, (i + 1) * 128)
            y_box[op, 0, i // 4, i % 4] = tiles[:SHARE, lanes].astype(BF16)
            y_box[op, 0, i // 4, 4 + i % 4] = tiles[SHARE:, lanes].astype(BF16)
        if products:
            tile = split(column_sums(products))
            for peer in range(Y):
                y_box[op, 0, peer, Z] = tile

    def relay_turn(op):
        y_waits(0, op).wait_recv()
        for m in range(Z // 2):
            for pair, part in ((0, 0), (1, 0), (0, 1), (1, 1)):
                at = 4 * part + m
                one, two = regroup(y_box[op, 1, 2 * pair, at], y_box[op, 1, 2 * pair + 1, at])
                z_box[op, 0, 2 * m, 2 * part + pair] = one
                z_box[op, 0, 2 * m + 1, 2 * part + pair] = two
        if op == 1:
            tile = split(joined(y_box[1, 1, :, Z]))
            for peer in range(Z):
                z_box[1, 0, peer, Y] = tile
        along_z(0, op)

    def relay_in(op):
        z_waits(0, op).wait_recv()
        for i in range(OWN // 2):
            lanes = slice(i * 128, (i + 1) * 128)
            p_mat[:SHARE, lanes] = z_box[op, 1, i // 2, i % 2]
            p_mat[SHARE:, lanes] = z_box[op, 1, i // 2, 2 + i % 2]
        return p_mat[...]

    def return_out(op, tiles, products=()):
        for i in range(OWN // 2):
            tile = tiles[:, i * 128 : (i + 1) * 128]
            high = tile.astype(BF16)
            z_box[op, 2, i // 2, i % 2] = high
            z_box[op, 2, i // 2, 2 + i % 2] = (tile - high.astype(F32)).astype(BF16)
        if products:
            tile = split(column_sums(products))
            for peer in range(Z):
                z_box[op, 2, peer, Y] = tile
        along_z(1, op)

    def return_turn(op):
        z_waits(1, op).wait_recv()
        for m in range(Z // 2):
            for pair, part in ((0, 0), (1, 0), (0, 1), (1, 1)):
                at = 2 * part + pair
                one, two = regroup(z_box[op, 3, 2 * m, at], z_box[op, 3, 2 * m + 1, at])
                y_box[op, 2, 2 * pair, 4 * part + m] = one
                y_box[op, 2, 2 * pair + 1, 4 * part + m] = two
        if op == 1:
            tile = split(joined(z_box[1, 3, :, Y]))
            for peer in range(Y):
                y_box[1, 2, peer, Z] = tile
        along_y(1, op)

    def return_in(op):
        y_waits(1, op).wait_recv()
        for i in range(OWN // 2):
            lanes = slice(i * 128, (i + 1) * 128)
            p_mat[:SHARE, lanes] = y_box[op, 3, i // 4, i % 4]
            p_mat[SHARE:, lanes] = y_box[op, 3, i // 4, 4 + i % 4]
        return p_mat[...]

    def fold(both):
        return both[:SHARE] + both[SHARE:]

    def make_send_hot():
        at = lax.broadcasted_iota(jnp.int32, (ROWS, 2 * SLOTS), 0)
        for peer in range(Y):
            even = rows[pl.ds(peer, Z // 2, stride=2 * Y), :]
            odd = rows[pl.ds(peer + Y, Z // 2, stride=2 * Y), :]
            pairs = jnp.concatenate([even, odd], axis=1)
            for m in range(Z // 2):
                lanes = slice((peer * 4 + m) * 128, (peer * 4 + m + 1) * 128)
                send_hot[:, lanes] = (at == pairs[m : m + 1, :]).astype(F32).astype(BF16)

    def make_parent_hot():
        def some(i, carry):
            at = lax.broadcasted_iota(jnp.int32, (128, ROWS), 0) + i * 128
            here = (at == sire[...]) | (at == dam[...])
            parent_hot[pl.ds(pl.multiple_of(i * 128, 128), 128), :] = here.astype(F32).astype(BF16)
            return carry

        lax.fori_loop(0, OWN * SLOTS // 128, some, 0)

    def pedigree_out(op, value, products=()):
        relay_out(op, dot(halves(value), send_hot[...]), products)

    def pedigree_mid(op, value):
        parents = fold(dot(relay_in(op), parent_hot[...]))
        lacks = value - 0.5 * parents
        return lacks, mend[...] * lacks

    def pedigree_back(op, value, lacks, term):
        back = -0.5 * fold(dot_nt(halves(term), parent_hot[...]))
        if op == 0:
            return_out(op, back)
            return ()
        gamma, delta, square = joined(z_box[1, 1, :, Y])
        alpha = gamma / delta
        rest = b_share - alpha * value
        return_out(
            op, back, (rest * rest, rest * value, d_share * value * value + term * lacks)
        )
        return gamma, alpha, square, rest

    def pedigree_end(op, term):
        return term + fold(dot_nt(return_in(op), send_hot[...]))

    def share_field(value):
        field[1, mine, :] = value.astype(BF16)

        def give(k, carry):
            piece = field.at[1, mine, :]
            remote(piece, piece, x_s, x_r, at_s(k)).start()
            return carry

        lax.fori_loop(1, S, give, 0)

    def field_arrives():
        settle(field.at[1, 0 : COLS - SHARE, :], x_s, x_r, at_s(1)).wait_recv()

    def to_snp(ref, send_sem, recv_sem):
        def give(k, carry):
            piece = ref.at[mine, :]
            remote(piece, piece, send_sem, recv_sem, at_s(k)).start()
            return carry

        lax.fori_loop(1, S, give, 0)

    def all_of(ref, send_sem, recv_sem):
        return settle(ref.at[0 : COLS - SHARE, :], send_sem, recv_sem, at_s(1))

    for sub in range(SUBS):
        effects_out(0, sub, send=False)
    make_send_hot()
    pedigree_out(0, b_share)
    pl.semaphore_wait(barrier, Y - 1 + Z - 1 + S - 1)
    turn_out(0)
    effects_send(0, 0)
    along_y(0, 0)
    effects_send(0, 1)
    make_parent_hot()
    diag_t[...] = diag[...].T
    d_share = diag_t[mine, :]
    effects_mid(0, 0)
    effects_send(0, 2)
    relay_turn(0)
    effects_mid(0, 1)
    turn_mid(0)
    effects_mid(0, 2)
    effects_sum(0, 0)
    lacks, term = pedigree_mid(0, b_share)
    effects_sum(0, 1)
    turn_sum(0)
    pedigree_back(0, b_share, lacks, term)
    effects_spread(0, 0)
    effects_sum(0, 2)
    turn_spread(0)
    effects_spread(0, 1)
    return_turn(0)
    effects_spread(0, 2)
    take(0, 0)
    take(0, 1)
    take(0, 2)
    take(0, 3)
    genomic_out(0)
    ped = pedigree_end(0, term)
    w_share = d_share * b_share + ped
    w_share = w_share + scale * genomic_in(0)
    share_field(w_share)
    pedigree_out(1, w_share, (b_share * b_share, w_share * b_share, w_share * w_share))
    along_y(0, 1)
    w_full[mine, :] = w_share
    field_arrives()

    effects_out(1, 3, send=False)
    turn_out(1)
    effects_out(1, 0)
    effects_out(1, 1)
    effects_out(1, 2, send=False)
    relay_turn(1)
    effects_mid(1, 0)
    effects_send(1, 2)
    to_snp(w_full, w_s, w_r)
    effects_mid(1, 1)
    lacks, term = pedigree_mid(1, w_share)
    turn_mid(1)
    effects_mid(1, 2)
    effects_sum(1, 0)
    gamma0, alpha0, square0, r_share = pedigree_back(1, w_share, lacks, term)
    effects_sum(1, 1)
    turn_sum(1)
    effects_spread(1, 0)
    effects_sum(1, 2)
    turn_spread(1)
    return_turn(1)
    effects_spread(1, 1)
    effects_spread(1, 2)
    take(1, 0)
    take(1, 1)
    take(1, 2)
    take(1, 3)
    genomic_out(1)
    ped = pedigree_end(1, term)
    gamma1, cross, quad = joined(y_box[1, 3, :, Z])
    beta = gamma1 / gamma0
    quad = quad + scale * norm_in()
    delta1 = cross - alpha0 * (square0 - alpha0 * quad)
    alpha1 = gamma1 / (delta1 - beta * gamma1 / alpha0)
    scalars[mine, :] = pack(alpha0, beta, alpha1)
    to_snp(scalars, c_s, c_r)
    q_share = d_share * w_share + ped + scale * genomic_in(1)
    w1_share = w_share - alpha0 * q_share
    result[mine, :] = (r_share - alpha1 * (w1_share + beta * w_share)).astype(BF16)
    to_snp(result, f_s, f_r)
    all_of(w_full, w_s, w_r).wait()
    all_of(scalars, c_s, c_r).wait()
    alpha0, beta, alpha1 = (scalars[:, i : i + 1] for i in range(3))
    b_full = field_t[...]
    x_out[...] = (
        alpha0 * b_full + alpha1 * ((b_full - alpha0 * w_full[...]) + beta * b_full)
    ).T
    all_of(result, f_s, f_r).wait()
    r_out[...] = result[...].astype(F32).T

    for op in range(2):
        settle(turn_recv.at[op, 0 : Z - 1], tz_s.at[op], tz_r.at[op], at_z(1)).wait_send()
        settle(turn_end.at[op, 0 : Y - 1], ty_s.at[op], ty_r.at[op], at_y(1)).wait_send()
        turn_rows(op).wait_send()
        turn_all(op).wait_send()
        for sub in range(LAST):
            here = spot(sub)
            for k in range(1, Y):
                settle(
                    y_send.at[op, :, y_lanes(0, sub)], y_s.at[op, k - 1, sub], y_r.at[op, 0, sub], at_y(k)
                ).wait_send()
                settle(
                    effects.at[op, :, y_lanes(y, sub)],
                    yg_s.at[op, k - 1, sub], yg_r.at[op, 0, sub], at_y(k),
                ).wait_send()
            settle(
                z_send.at[op, 0 : COLS - ZSHARE, here], z_s.at[op, sub], z_r.at[op, sub], at_z(1)
            ).wait_send()
            settle(
                effects.at[op, 0 : COLS - ZSHARE, y_lanes(y, sub)],
                zg_s.at[op, sub], zg_r.at[op, sub], at_z(1),
            ).wait_send()
        settle(g_send.at[op, 0 : COLS - SHARE, :], g_s.at[op], g_r.at[op], at_s(1)).wait_send()
        for leg in range(2):
            y_waits(leg, op).wait_send()
            z_waits(leg, op).wait_send()
    settle(field.at[1, 0 : COLS - SHARE, :], x_s, x_r, at_s(1)).wait_send()
    settle(norm_recv.at[0 : S - 1], n_s, n_r, at_s(1)).wait_send()


def put_out(x, r, x_out, r_out):
    x_out[...] = x[...]
    r_out[...] = r[...]


def local(geno, freq, rhs, diag, mend, weight, send_rows, sire, dam):
    vmem = pl.BlockSpec(memory_space=pltpu.VMEM)
    dma = pltpu.SemaphoreType.DMA
    results = pl.pallas_call(
        kernel,
        out_shape=(jax.ShapeDtypeStruct((ROWS, COLS), F32),) * 2,
        in_specs=[pl.BlockSpec(memory_space=pl.ANY)] + [vmem] * 8,
        out_specs=(vmem, vmem),
        scratch_shapes=[
            pltpu.VMEM((ROWS, LOCAL), BF16),
            pltpu.VMEM((ROWS, OWN * SLOTS), BF16),
            pltpu.VMEM((OWN * SLOTS, ROWS), BF16),
            pltpu.VMEM((2, COLS, ROWS), BF16),
            pltpu.VMEM((COLS, ROWS), F32),
            pltpu.VMEM((COLS, ROWS), F32),
            pltpu.VMEM((COLS, LOCAL), F32),
            pltpu.VMEM((2, COLS, LOCAL), BF16),
            pltpu.VMEM((2, Y, COLS, YCH), BF16),
            pltpu.VMEM((COLS, YCH), F32),
            pltpu.VMEM((2, COLS, YCH), BF16),
            pltpu.VMEM((2, Z, ZSHARE, YCH), BF16),
            pltpu.VMEM((2, COLS, LOCAL), BF16),
            pltpu.VMEM((COLS, ROWS), F32),
            pltpu.VMEM((2, COLS, ROWS), BF16),
            pltpu.VMEM((2, S, SHARE, ROWS), BF16),
            pltpu.VMEM((2, 4, Y, Z + 1, SHARE, 2 * SLOTS), BF16),
            pltpu.VMEM((2, 4, Z, Y + 1, SHARE, 2 * SLOTS), BF16),
            pltpu.VMEM((2 * SHARE, OWN * SLOTS), BF16),
            pltpu.VMEM((COLS, ROWS), F32),
            pltpu.VMEM((COLS, ROWS), BF16),
            pltpu.VMEM((COLS, 128), F32),
            pltpu.VMEM((COLS, 128), F32),
            pltpu.VMEM((COLS, 128), F32),
            pltpu.VMEM((S, SHARE, 128), F32),
            pltpu.VMEM((2, Z, ZSHARE, YCH), BF16),
            pltpu.VMEM((ZSHARE, YCH), F32),
            pltpu.VMEM((2, ZSHARE, YCH), BF16),
            pltpu.VMEM((2, Y, ZSHARE, SUB), BF16),
            dma((SUBS,)),
            dma((2, Y - 1, SUBS)), dma((2, Y, SUBS)),
            dma((2, SUBS)), dma((2, SUBS)),
            dma((2, SUBS)), dma((2, SUBS)),
            dma((2, Y - 1, SUBS)), dma((2, Y, SUBS)),
            dma((2,)), dma((2,)),
            dma, dma,
            dma((2, 2)), dma((2, 2)),
            dma, dma,
            dma, dma,
            dma, dma,
            dma, dma,
            dma((2, 2)), dma((2, 2)),
            *[dma((2,))] * 8,
        ],
        compiler_params=pltpu.CompilerParams(
            collective_id=0, has_side_effects=True, vmem_limit_bytes=56 * 2**20
        ),
        cost_estimate=pl.CostEstimate(
            flops=5_000_000_000, bytes_accessed=12_000_000, transcendentals=0
        ),
    )(
        geno,
        freq.reshape(1, LOCAL),
        rhs,
        diag,
        mend.reshape(1, ROWS),
        weight.reshape(1, COLS),
        send_rows[0],
        sire.reshape(1, ROWS),
        dam.reshape(1, ROWS),
    )
    half = pl.BlockSpec((ROWS // 2, COLS), lambda i: (i, 0))
    return pl.pallas_call(
        put_out,
        grid=(2,),
        out_shape=(jax.ShapeDtypeStruct((ROWS, COLS), F32),) * 2,
        in_specs=[half] * 2,
        out_specs=(half,) * 2,
    )(*results)


def solution(mesh):
    placed = (
        P("animal", "snp"),
        P("snp"),
        P("animal", None),
        P("animal", None),
        P("animal"),
        P(),
        P("animal", None, None),
        P("animal"),
        P("animal"),
    )
    return jax.shard_map(
        local,
        mesh=mesh,
        in_specs=placed,
        out_specs=(P("animal", None), P("animal", None)),
        check_vma=False,
    )
```
